256 devices in a mesh: seq: 4 (over y), expert: 64 (over x, z, core).
Axes of the slice: x: 4, y: 4, z: 8, core: 2. Of those that a mesh axis runs over, the one named last changes fastest.
Arguments:
- decoder_states: bfloat16 [64, 512, 1024], P('expert', 'seq'), may hold values from -8 to 8
- queries: bfloat16 [64, 512, 1024], P('expert', 'seq'), may hold values from -5 to 5
- encoder_keys: bfloat16 [64, 512, 1024], P('expert', 'seq'), may hold values from -5 to 5
- encoder_values: bfloat16 [64, 512, 1024], P('expert', 'seq'), may hold values from -6 to 6
- source_lengths: int32 [64], P('expert'), may hold values from 256 to 512
- norm_gain: float32 [1024], replicated, may hold values from 0.5 to 1.5
- router_weight: bfloat16 [1024, 64], replicated, may hold values from -0.1875 to 0.1875
- expert_ids: int32 [64, 512, 2], P('expert', 'seq'), may hold values from 0 to 63, all different within a row; in each aligned block of 128 rows (0 to 127, 128 to 255, ..., all dimensions but the last counted through in order) at most 6 rows name the same one
- expert_in: bfloat16 [64, 4096, 1024], P('expert', 'seq'), may hold values from -0.1875 to 0.1875
- expert_out: bfloat16 [64, 4096, 1024], P('expert', 'seq'), may hold values from -0.09375 to 0.09375
- grad_output: bfloat16 [64, 512, 1024], P('expert', 'seq'), may hold values from -6 to 6
Outputs:
- layer_output: bfloat16 [64, 512, 1024], P('expert', 'seq')
- grad_states: bfloat16 [64, 512, 1024], P('expert', 'seq')
- grad_queries: bfloat16 [64, 512, 1024], P('expert', 'seq')
- grad_keys: float32 [64, 512, 1024], P('expert', 'seq')
- grad_values: float32 [64, 512, 1024], P('expert', 'seq')
The draws below stay inside these ranges and needn't reach their ends.
Inputs may be any that keep to these rules, and one draw needn't show every extreme that they name: `expert_ids`: the two experts of a position differ; among the 128 positions of one device (aligned blocks of the flattened sequence positions) no expert is named more than 6 times, a bound that some block reaches.
All inputs are finite; a program needn't handle non-finite values.
Results may differ from the reference program's by a relative error of at most 0.024.
Values may be sent and summed in bfloat16 or wider, within the bound.
A program may use at most 128 MiB of HBM per device.

```python
import math
import jax
import jax.numpy as jnp
import numpy as np
from jax import lax

TOK_DEV = 128
H = 8
HD = 128
D = 1024
FF = 4096
EXPERTS = 64
SEQS = 64
DEC = 512
SRC = 512
C = 6
N_SEQ = 4


def draw_queries(key, part):
    noise_key = jax.random.fold_in(key, 11)
    result = jnp.clip(jax.random.normal(noise_key, (SEQS, DEC, D), jnp.float32), -5.0, 5.0)
    return result.astype(jnp.bfloat16)


def draw_encoder_keys(key, part):
    noise_key = jax.random.fold_in(key, 21)
    result = jnp.clip(jax.random.normal(noise_key, (SEQS, SRC, D), jnp.float32), -5.0, 5.0)
    return result.astype(jnp.bfloat16)


def draw_decoder_states(key, part):
    base_key, row_key, column_key = jax.random.split(jax.random.fold_in(key, 31), 3)
    background = jnp.clip(jax.random.normal(base_key, (SEQS, DEC, D), jnp.float32), -4.0, 4.0)
    row_scale = jnp.exp(jax.random.uniform(row_key, (SEQS, DEC, 1), jnp.float32, math.log(0.1), math.log(1.0)))
    column_scale = jnp.exp(jax.random.uniform(column_key, (1, 1, D), jnp.float32, math.log(0.3), math.log(3.0)))
    return jnp.clip(background * row_scale * column_scale, -8.0, 8.0).astype(jnp.bfloat16)


def with_ends(values, stream_key, smallest, high):
    longest = values.shape.index(max(values.shape))
    spots = []
    for shift in (0, 1):
        where = [jax.random.randint(jax.random.fold_in(stream_key, axis), (), 0, length) for axis, length in enumerate(values.shape)]
        where[longest] = (where[longest] + shift) % values.shape[longest]
        spots.append(tuple(where))
    return values.at[spots[0]].set(smallest).at[spots[1]].set(high)


def block_levels(rng, dims, shards, least, top_value):
    level = 1.0
    for position, shards_of in shards:
        draws = jax.random.uniform(jax.random.fold_in(jax.random.fold_in(rng, 6), position), (shards_of,), jnp.float32, least / len(shards), top_value / len(shards))
        level = level * jnp.repeat(jnp.exp(draws), dims[position] // shards_of).reshape((-1,) + (1,) * (len(dims) - 1 - position))
    return level


def shared_out(own_key, own, number, rows, amount, top, bound, skew):
    order = jax.random.permutation(own_key, amount)
    packed, usual = portions_of(amount, rows * top, bound, skew, True), portions_of(amount, rows * top, bound, skew, False)
    places = jnp.arange(amount)

    def named(tallies, rotation):
        used = int((tallies > 0).sum())
        fixed = max(1, used // 4)
        passed = fixed + (places - fixed + rotation * (used - fixed)) % max(1, amount - fixed)
        return jnp.zeros((amount,), jnp.int32).at[order[jnp.where(places < fixed, places, passed)]].set(jnp.asarray(tallies, jnp.int32))

    tallies = jnp.where(number % 4 == 0, named(packed, number // 4), named(usual, number - number // 4 - 1))
    mixed = jax.random.permutation(jax.random.fold_in(own, 3), amount)
    donor, receiver = mixed[0:amount // 2 * 2:2], mixed[1:amount // 2 * 2:2]
    margin = jnp.minimum(tallies[donor] - 1, bound - tallies[receiver]) // 2
    margin = jnp.where((donor == order[0]) | (receiver == order[0]) | (tallies[receiver] == 0), 0, jnp.maximum(margin, 0))
    passed = jax.random.randint(jax.random.fold_in(own, 4), (amount // 2,), 0, 1 << 20) % (margin + 1)
    tallies = tallies.at[donor].add(-passed).at[receiver].add(passed)
    members = jnp.searchsorted(jnp.cumsum(tallies), jnp.arange(rows * top), side="right").astype(jnp.int32)
    table = members.reshape(top, rows).T
    table = table[jax.random.permutation(jax.random.fold_in(own, 1), rows)]
    rotation = jax.random.randint(jax.random.fold_in(own, 2), (rows, 1), 0, top)
    return jnp.take_along_axis(table, (jnp.arange(top)[None, :] + rotation) % top, axis=1)


def portions_of(count, total, bound, lean, full):
    portions = [(1 << 20) // math.isqrt(rank ** lean) + 1 for rank in range(1, count + 1)]
    largest = bound if full else min(bound, max(-(-total // count), total * portions[0] // sum(portions)))
    least = 1 if total - largest >= count - 1 else 0
    given, surplus = [largest] + [least] * (count - 1), total - largest - least * (count - 1)
    while surplus > 0:
        free = [i for i in range(1, count) if given[i] < largest] or [i for i in range(1, count) if given[i] < bound]
        whole, remaining = sum([portions[i] for i in free]), surplus
        for i in free:
            extra = min(bound - given[i], max(1, remaining * portions[i] // whole), surplus)
            given[i] = given[i] + extra
            surplus = surplus - extra
    return np.array(given)


def scatter_about(rng, extent, deviation, bound, cuts=(), kind=jnp.bfloat16):
    loudness = block_levels(rng, extent, cuts, -0.22, 0.18) if cuts else 1.0
    array = jax.random.normal(rng, extent, jnp.float32) * deviation * loudness
    return jnp.minimum(jnp.maximum(array, -bound), bound).astype(kind)


def setup_inputs(seed: int = 0) -> dict:
    arg_keys = jax.random.split(jax.random.key(seed), 12)
    decoder_states = draw_decoder_states(jax.random.fold_in(arg_keys[11], 71), 0)
    queries = draw_queries(jax.random.fold_in(arg_keys[11], 71), 0)
    encoder_keys = draw_encoder_keys(jax.random.fold_in(arg_keys[11], 71), 0)
    encoder_values = scatter_about(arg_keys[3], (SEQS, SRC, D), 1.0, 6.0, ((0, 64), (1, 4)))
    source_lengths = with_ends(jax.random.randint(arg_keys[4], (SEQS,), SRC // 2, SRC + 1), jax.random.fold_in(arg_keys[4], 1), SRC // 2, SRC).astype(jnp.int32)
    norm_gain = jnp.clip(1.0 + 0.1 * jax.random.normal(arg_keys[5], (D,), jnp.float32), 0.5, 1.5)
    router_weight = scatter_about(arg_keys[6], (D, EXPERTS), D ** -0.5, 0.1875)
    expert_ids_keys = jax.random.split(jax.random.fold_in(arg_keys[7], 1), SEQS * DEC // TOK_DEV)
    expert_ids_turns = jax.random.permutation(jax.random.fold_in(arg_keys[7], 3), SEQS * DEC // TOK_DEV)
    expert_ids = jax.vmap(lambda own, number: shared_out(jax.random.fold_in(arg_keys[7], 2), own, number, TOK_DEV, EXPERTS, 2, C, 2))(expert_ids_keys, expert_ids_turns).reshape((SEQS, DEC, 2))
    expert_in = scatter_about(arg_keys[8], (EXPERTS, FF, D), D ** -0.5, 0.1875, ((0, 64), (1, 4)))
    expert_out = scatter_about(arg_keys[9], (EXPERTS, FF, D), FF ** -0.5, 0.09375, ((0, 64), (1, 4)))
    grad_output = scatter_about(arg_keys[10], (SEQS, DEC, D), 1.0, 6.0, ((0, 64), (1, 4)))
    return dict(decoder_states=decoder_states, queries=queries, encoder_keys=encoder_keys, encoder_values=encoder_values, source_lengths=source_lengths, norm_gain=norm_gain, router_weight=router_weight, expert_ids=expert_ids, expert_in=expert_in, expert_out=expert_out, grad_output=grad_output)


gelu_scale = 0.7978845608028654
cubic_weight = 0.044715

def gelu_curve(signal):
    inner = gelu_scale * (signal + cubic_weight * signal * signal * signal)
    return 0.5 * signal * (1.0 + jnp.tanh(inner))

def gelu_slope(signal):
    tangent = jnp.tanh(gelu_scale * (signal + cubic_weight * signal * signal * signal))
    return 0.5 * (1.0 + tangent) + 0.5 * signal * (1.0 - tangent * tangent) * gelu_scale * (1.0 + 3.0 * cubic_weight * signal * signal)

def rounded(tensor):
    return lax.optimization_barrier(tensor.astype(jnp.bfloat16)).astype(jnp.float32)

def attend(query_rows, key_rows, value_rows, length):
    score_scale = 1.0 / math.sqrt(HD)
    query_heads = query_rows.astype(jnp.float32).reshape(DEC, H, HD)
    key_heads = key_rows.astype(jnp.float32).reshape(SRC, H, HD)
    value_heads = value_rows.astype(jnp.float32).reshape(SRC, H, HD)
    scores = jnp.einsum('thd,khd->htk', query_heads, key_heads) * score_scale
    key_valid = jnp.arange(SRC, dtype=jnp.int32) < length
    scores = jnp.where(key_valid[None, None, :], scores, -1e+30)
    row_max = lax.optimization_barrier(jnp.max(scores, axis=-1, keepdims=True))
    raw_weights = jnp.exp(scores - row_max)
    probability = raw_weights / lax.optimization_barrier(jnp.sum(raw_weights, axis=-1, keepdims=True))
    rounded_prob = rounded(probability)
    context = jnp.einsum('htk,khd->thd', rounded_prob, value_heads).reshape(DEC, D)
    return (probability, rounded_prob, context, query_heads, key_heads, value_heads)

def forward_context(operands):
    return attend(operands[0], operands[1], operands[2], operands[3])[2]

def attention_grads(operands):
    query_rows, key_rows, value_rows, length, grad_rows = operands
    score_scale = 1.0 / math.sqrt(HD)
    probability, rounded_prob, context, query_heads, key_heads, value_heads = attend(query_rows, key_rows, value_rows, length)
    grad_heads = grad_rows.astype(jnp.float32).reshape(DEC, H, HD)
    grad_probability = jnp.einsum('thd,khd->htk', grad_heads, value_heads)
    row_inner = lax.optimization_barrier(jnp.sum(probability * grad_probability, axis=-1, keepdims=True))
    grad_scores = rounded(probability * (grad_probability - row_inner))
    grad_queries = (jnp.einsum('htk,khd->thd', grad_scores, key_heads) * score_scale).reshape(DEC, D).astype(jnp.bfloat16)
    score_blocks = grad_scores.reshape(H, N_SEQ, TOK_DEV, SRC)
    weight_blocks = rounded_prob.reshape(H, N_SEQ, TOK_DEV, SRC)
    query_blocks = query_heads.reshape(N_SEQ, TOK_DEV, H, HD)
    grad_blocks = grad_heads.reshape(N_SEQ, TOK_DEV, H, HD)
    key_terms = jnp.einsum('hjtk,jthd->jkhd', score_blocks, query_blocks) * score_scale
    value_terms = jnp.einsum('hjtk,jthd->jkhd', weight_blocks, grad_blocks)
    key_total = lax.optimization_barrier(jnp.sum(rounded(key_terms), axis=0)).reshape(SRC, D)
    value_total = lax.optimization_barrier(jnp.sum(rounded(value_terms), axis=0)).reshape(SRC, D)
    return (grad_queries, key_total, value_total)

def expert_step(operands):
    rows_in, grad_in, weight_in, weight_out = operands
    hidden_slice = FF // N_SEQ
    hidden_in = jnp.dot(rows_in, weight_in.T, preferred_element_type=jnp.float32)
    hidden = gelu_curve(hidden_in).astype(jnp.bfloat16)
    grad_hidden = (jnp.dot(grad_in, weight_out.T, preferred_element_type=jnp.float32) * gelu_slope(hidden_in)).astype(jnp.bfloat16)
    outputs = jnp.zeros((rows_in.shape[0], D), jnp.float32)
    grad_total = jnp.zeros((rows_in.shape[0], D), jnp.float32)
    for piece_index in range(N_SEQ):
        low_edge = piece_index * hidden_slice
        high_edge = low_edge + hidden_slice
        part_out = jnp.dot(hidden[:, low_edge:high_edge], weight_out[low_edge:high_edge], preferred_element_type=jnp.float32)
        part_grad = jnp.dot(grad_hidden[:, low_edge:high_edge], weight_in[low_edge:high_edge], preferred_element_type=jnp.float32)
        outputs = outputs + rounded(part_out)
        grad_total = grad_total + rounded(part_grad)
    return (outputs.astype(jnp.bfloat16), grad_total.astype(jnp.bfloat16))

def reference(decoder_states, queries, encoder_keys, encoder_values, source_lengths, norm_gain, router_weight, expert_ids, expert_in, expert_out, grad_output):
    token_total = SEQS * DEC
    block_count = SEQS * N_SEQ
    row_total = block_count * C
    context = lax.map(forward_context, (queries, encoder_keys, encoder_values, source_lengths))
    residual = (decoder_states.astype(jnp.float32) + context).reshape(token_total, D)
    centred = residual - lax.optimization_barrier(jnp.mean(residual, axis=-1, keepdims=True))
    reciprocal = 1.0 / jnp.sqrt(lax.optimization_barrier(jnp.mean(centred * centred, axis=-1, keepdims=True)) + 1e-05)
    normed = centred * reciprocal
    routed_in = (normed * norm_gain).astype(jnp.bfloat16)
    logits = jnp.dot(routed_in, router_weight, preferred_element_type=jnp.float32)
    chosen_experts = expert_ids.reshape(token_total, 2)
    expert_iota = jnp.arange(EXPERTS, dtype=jnp.int32)
    first_hot = chosen_experts[:, 0:1] == expert_iota[None, :]
    second_hot = chosen_experts[:, 1:2] == expert_iota[None, :]
    first_logit = lax.optimization_barrier(jnp.sum(jnp.where(first_hot, logits, 0.0), axis=-1))
    second_logit = lax.optimization_barrier(jnp.sum(jnp.where(second_hot, logits, 0.0), axis=-1))
    gates = jnp.stack([1.0 / (1.0 + jnp.exp(second_logit - first_logit)), 1.0 / (1.0 + jnp.exp(first_logit - second_logit))], axis=1)
    pair_hot = (chosen_experts.reshape(block_count, 2 * TOK_DEV)[:, :, None] == expert_iota[None, None, :]).astype(jnp.int32)
    running = jnp.cumsum(pair_hot, axis=1)
    slot_rank = lax.optimization_barrier(jnp.sum(running * pair_hot, axis=-1)) - 1
    block_start = jnp.arange(block_count, dtype=jnp.int32)[:, None] * C
    slot_index = (slot_rank + block_start).reshape(token_total, 2).astype(jnp.int32)
    cotangent = grad_output.reshape(token_total, D).astype(jnp.float32)
    slot_grads = (gates[:, :, None] * cotangent[:, None, :]).astype(jnp.bfloat16)
    send_rows = jnp.zeros((EXPERTS, row_total, D), jnp.bfloat16).at[chosen_experts, slot_index].set(jnp.broadcast_to(routed_in[:, None, :], (token_total, 2, D)))
    grad_rows = jnp.zeros((EXPERTS, row_total, D), jnp.bfloat16).at[chosen_experts, slot_index].set(slot_grads)
    results, grad_results = lax.map(expert_step, (send_rows, grad_rows, expert_in, expert_out))
    expert_outs = results[chosen_experts, slot_index].astype(jnp.float32)
    layer_output = residual + lax.optimization_barrier(jnp.sum(gates[:, :, None] * expert_outs, axis=1))
    gate_grads = lax.optimization_barrier(jnp.sum(cotangent[:, None, :] * expert_outs, axis=-1))
    gate_mean = lax.optimization_barrier(jnp.sum(gates * gate_grads, axis=-1, keepdims=True))
    logit_parts = gates * (gate_grads - gate_mean)
    logit_grads = jnp.where(first_hot, logit_parts[:, 0:1], 0.0) + jnp.where(second_hot, logit_parts[:, 1:2], 0.0)
    grad_routed = lax.optimization_barrier(jnp.sum(grad_results[chosen_experts, slot_index].astype(jnp.float32), axis=1))
    grad_routed = grad_routed + jnp.dot(logit_grads, router_weight.astype(jnp.float32).T, precision=lax.Precision.HIGHEST)
    grad_norm = grad_routed * norm_gain
    grad_residual = cotangent + reciprocal * (grad_norm - lax.optimization_barrier(jnp.mean(grad_norm, axis=-1, keepdims=True)) - normed * lax.optimization_barrier(jnp.mean(grad_norm * normed, axis=-1, keepdims=True)))
    grad_states = grad_residual.astype(jnp.bfloat16).reshape(SEQS, DEC, D)
    grad_queries, grad_keys, grad_values = lax.map(attention_grads, (queries, encoder_keys, encoder_values, source_lengths, grad_states))
    return (layer_output.astype(jnp.bfloat16).reshape(SEQS, DEC, D), grad_states, grad_queries, grad_keys, grad_values)
```

```python
import functools
import math

import jax
import jax.numpy as jnp
import numpy as np
from jax import lax
from jax.experimental import pallas as pl
from jax.experimental.pallas import tpu as pltpu
from jax.sharding import PartitionSpec as P

H = 8
HD = 128
CAP = 6
SIDE = 8
GROUP = SIDE * CAP
SLOTS = SIDE * GROUP
MESH = pl.DeviceIdType.MESH
F32 = jnp.float32
BF16 = jnp.bfloat16

gelu_scale = 0.7978845608028654
cubic_weight = 0.044715

KV, GR, XR = 0, 1, 2
RG, RO, RKV = 0, 1, 2
AG, AX, BG, BO = 0, 1, 2, 3


def dot_nn(a, b):
    return lax.dot_general(a, b, (((1,), (0,)), ((), ())), preferred_element_type=F32)


def dot_nt(a, b):
    return lax.dot_general(a, b, (((1,), (1,)), ((), ())), preferred_element_type=F32)


def dot_tn(a, b):
    return lax.dot_general(a, b, (((0,), (0,)), ((), ())), preferred_element_type=F32)


def layer(
    length_ref,
    dec_ref,
    q_ref,
    k_ref,
    v_ref,
    gain_ref,
    router_ref,
    ids_ref,
    win_ref,
    wout_ref,
    gout_ref,
    swap_ref,
    layer_ref,
    gstates_ref,
    gq_ref,
    gk_ref,
    gv_ref,
    kvb,
    win,
    wout,
    xg,
    gg,
    send,
    zbuf,
    turned,
    pick,
    prob,
    residual,
    normed,
    hid,
    ghd,
    part,
    opp,
    near_l,
    near_r,
    kpart,
    kopp,
    knear_l,
    knear_r,
    back_x,
    local_sem,
    ag_s,
    ag_r,
    rs_s,
    rs_r,
    xs_s,
    xs_r,
):
    tokens, width = dec_ref.shape
    half = width // 2
    ny = lax.axis_size("seq")
    y = lax.axis_index("seq")
    e = lax.axis_index("expert")
    core = lax.rem(e, 2)
    z = lax.rem(e // 2, SIDE)
    x = e // (2 * SIDE)
    xc = x * 2 + core
    right = (lax.rem(y + 1, ny), e)
    left = (lax.rem(y + ny - 1, ny), e)
    hops = (4, 3, 5, 2, 6, 1, 7)

    def z_peer(hop):
        there = lax.rem(z + hop, SIDE)
        return there, (y, x * (2 * SIDE) + there * 2 + core)

    def xc_peer(hop):
        there = lax.rem(xc + hop, SIDE)
        return there, (y, (there // 2) * (2 * SIDE) + z * 2 + lax.rem(there, 2))

    def remote(src, dst, s, r, device):
        return pltpu.make_async_remote_copy(
            src_ref=src, dst_ref=dst, send_sem=s, recv_sem=r, device_id=device, device_id_type=MESH
        )

    own_k = pltpu.make_async_copy(k_ref, kvb.at[0, 0], local_sem.at[0])
    own_v = pltpu.make_async_copy(v_ref, kvb.at[0, 1], local_sem.at[1])
    own_in = pltpu.make_async_copy(win_ref, win, local_sem.at[2])
    own_out = pltpu.make_async_copy(wout_ref, wout, local_sem.at[3])
    for copy in (own_k, own_v, own_in, own_out):
        copy.start()

    barrier = pltpu.get_barrier_semaphore()
    for device in (left, right):
        pl.semaphore_signal(barrier, inc=1, device_id=device, device_id_type=MESH)
    for hop in hops:
        pl.semaphore_signal(barrier, inc=1, device_id=z_peer(hop)[1], device_id_type=MESH)
        pl.semaphore_signal(barrier, inc=1, device_id=xc_peer(hop)[1], device_id_type=MESH)
    pl.semaphore_wait(barrier, 2 + 2 * len(hops))

    class Gather:
        def __init__(self, number, buf, sources):
            def at(i):
                return ag_s.at[number * 6 + i], ag_r.at[number * 6 + i]

            self.to_right = [remote(sources[h], buf.at[3, h], *at(h), right) for h in (0, 1)]
            self.to_left = [remote(sources[h], buf.at[1, h], *at(2 + h), left) for h in (0, 1)]
            self.on_right = remote(buf.at[3, 0], buf.at[2, 0], *at(4), right)
            self.on_left = remote(buf.at[1, 1], buf.at[2, 1], *at(5), left)

        def forward_right(self):
            self.to_right[0].wait_recv()
            self.on_right.start()

        def forward_left(self):
            self.to_left[1].wait_recv()
            self.on_left.start()

        def sent(self):
            for copy in (*self.to_right, *self.to_left, self.on_right, self.on_left):
                copy.wait_send()

    class Reduce:
        def __init__(self, number, parts, across, from_left, from_right):
            def at(i):
                return rs_s.at[number * 6 + i], rs_r.at[number * 6 + i]

            self.parts, self.across = parts, across
            self.left_a = remote(parts.at[3, 0], from_right.at[0], *at(0), left)
            self.right_b = remote(parts.at[1, 1], from_left.at[1], *at(1), right)
            self.opposite_a = remote(parts.at[2, 0], across.at[0], *at(2), right)
            self.opposite_b = remote(parts.at[2, 1], across.at[1], *at(3), left)
            self.right_a = remote(parts.at[1, 0], from_left.at[0], *at(4), right)
            self.left_b = remote(parts.at[3, 1], from_right.at[1], *at(5), left)

        def pass_on(self):
            self.opposite_a.wait_recv()
            self.parts[1, 0] = (self.parts[1, 0].astype(F32) + self.across[0].astype(F32)).astype(BF16)
            self.right_a.start()
            self.opposite_b.wait_recv()
            self.parts[3, 1] = (self.parts[3, 1].astype(F32) + self.across[1].astype(F32)).astype(BF16)
            self.left_b.start()

        def arrived(self):
            for copy in (self.left_a, self.right_b, self.right_a, self.left_b):
                copy.wait_recv()

        def sent(self):
            for copy in (self.left_a, self.right_b, self.opposite_a, self.opposite_b, self.right_a, self.left_b):
                copy.wait_send()

    class Stage:
        def __init__(self, number, src, dst, peer, mine):
            self.s, self.r = xs_s.at[number], xs_r.at[number]
            self.src, self.dst, self.peer, self.mine = src, dst, peer, mine

        def rows(self, at):
            return pl.ds(pl.multiple_of(at * GROUP, 16), GROUP)

        def start(self):
            own = self.rows(self.mine)
            for hop in hops:
                there, device = self.peer(hop)
                remote(self.src.at[self.rows(there)], self.dst.at[own], self.s, self.r, device).start()
            pltpu.make_async_copy(self.src.at[own], self.dst.at[own], self.r).start()

        def arrived(self):
            pltpu.make_async_copy(self.src, self.dst, self.r).wait()

        def sent(self):
            most = pl.ds(0, SLOTS - GROUP)
            remote(self.src.at[most], self.dst.at[most], self.s, self.r, right).wait_send()

    def turn(src, dst):
        dst[...] = dot_nn(swap_ref[...], src[...]).astype(BF16)

    class Dispatch:
        def __init__(self, number, tensor, dst):
            self.first = [Stage(number * 4 + h, send.at[tensor, h], zbuf.at[tensor, h], z_peer, z) for h in (0, 1)]
            self.second = [Stage(number * 4 + 2 + h, turned.at[tensor, h], dst.at[h], xc_peer, xc) for h in (0, 1)]
            self.tensor = tensor

        def middle(self, h):
            self.first[h].arrived()
            turn(zbuf.at[self.tensor, h], turned.at[self.tensor, h])
            self.second[h].start()

        def sent(self):
            for stage in (*self.first, *self.second):
                stage.sent()

    class Return:
        def __init__(self, number, tensor, dst):
            self.first = [Stage(number * 4 + h, send.at[tensor, h], zbuf.at[tensor, h], xc_peer, xc) for h in (0, 1)]
            self.second = [Stage(number * 4 + 2 + h, turned.at[tensor, h], dst.at[h], z_peer, z) for h in (0, 1)]
            self.tensor = tensor

        middle = Dispatch.middle
        sent = Dispatch.sent

    keys = Gather(KV, kvb, (k_ref, v_ref))
    keys.to_right[0].start()
    keys.to_left[1].start()
    keys.to_right[1].start()
    keys.to_left[0].start()

    ids = ids_ref[...]
    experts = router_ref.shape[1]
    lanes = lax.broadcasted_iota(jnp.int32, (tokens, experts), 1)
    first_hot = ids[:, 0:1] == lanes
    second_hot = ids[:, 1:2] == lanes
    ones = first_hot.astype(F32), second_hot.astype(F32)
    earlier = (
        lax.broadcasted_iota(jnp.int32, (tokens, tokens), 0) > lax.broadcasted_iota(jnp.int32, (tokens, tokens), 1)
    ).astype(F32).astype(BF16)
    slot_lanes = lax.broadcasted_iota(jnp.int32, (tokens, SLOTS), 1)
    base = ((lanes // 2) % SIDE) * GROUP + (lanes // (2 * SIDE)) * (2 * CAP) + (lanes % 2) * CAP
    both = jnp.zeros((tokens, SLOTS), F32)
    for j in (0, 1):
        rank = dot_nn(earlier, ones[j].astype(BF16))
        if j == 1:
            rank = rank + jnp.sum(ones[0], axis=0, keepdims=True)
        slot = jnp.sum(ones[j] * (rank + base.astype(F32)), axis=-1, keepdims=True)
        chosen = (slot.astype(jnp.int32) == slot_lanes).astype(F32)
        pick[j] = chosen.astype(BF16)
        both = both + chosen
    spread = both.T.astype(BF16)
    for h in (0, 1):
        send[0, h] = dot_nn(spread, gout_ref[:, h * half : (h + 1) * half]).astype(BF16)

    grads = Dispatch(AG, 0, gg.at[0])
    grads.first[0].start()
    grads.first[1].start()
    keys.forward_right()
    keys.forward_left()
    grads.middle(0)
    grads.middle(1)
    keys.to_right[1].wait_recv()
    keys.to_left[0].wait_recv()
    own_k.wait()
    own_v.wait()
    keys.on_right.wait_recv()
    keys.on_left.wait_recv()

    score_scale = 1.0 / math.sqrt(HD)
    block_rows = kvb.shape[2]
    sources = ny * block_rows
    place = lax.broadcasted_iota(jnp.int32, (tokens, sources), 1)
    place = (place // block_rows + y) % ny * block_rows + place % block_rows
    valid = place < length_ref[0]

    def columns(head):
        return pl.ds(pl.multiple_of(head * HD, HD), HD)

    def attend(head, carry):
        at = columns(head)
        key_rows = kvb[:, 0, :, at].reshape(sources, HD)
        scores = dot_nt(q_ref[:, at], key_rows) * score_scale
        scores = jnp.where(valid, scores, -1e30)
        raw = jnp.exp(scores - jnp.max(scores, axis=-1, keepdims=True))
        probability = raw / jnp.sum(raw, axis=-1, keepdims=True)
        prob[head] = probability
        value_rows = kvb[:, 1, :, at].reshape(sources, HD)
        residual[:, at] = dec_ref[:, at].astype(F32) + dot_nn(probability.astype(BF16), value_rows)
        return carry

    lax.fori_loop(0, H, attend, 0)

    grad_rows = Gather(GR, gg, (gg.at[0, 0], gg.at[0, 1]))
    for h in (0, 1):
        grads.second[h].arrived()
        grad_rows.to_right[h].start()
        grad_rows.to_left[h].start()

    whole = residual[...]
    centred = whole - jnp.mean(whole, axis=-1, keepdims=True)
    reciprocal = 1.0 / jnp.sqrt(jnp.mean(centred * centred, axis=-1, keepdims=True) + 1e-05)
    normed[...] = centred * reciprocal
    routed_in = (normed[...] * gain_ref[...]).astype(BF16)
    for h in (0, 1):
        send[1, h] = dot_nn(spread, routed_in[:, h * half : (h + 1) * half]).astype(BF16)
    rows = Dispatch(AX, 1, xg.at[0])
    rows.first[0].start()
    rows.first[1].start()

    logits = dot_nn(routed_in, router_ref[...])
    first_logit = jnp.sum(jnp.where(first_hot, logits, 0.0), axis=-1, keepdims=True)
    second_logit = jnp.sum(jnp.where(second_hot, logits, 0.0), axis=-1, keepdims=True)
    gates = 1.0 / (1.0 + jnp.exp(second_logit - first_logit)), 1.0 / (1.0 + jnp.exp(first_logit - second_logit))

    grad_rows.forward_right()
    rows.middle(0)
    grad_rows.forward_left()
    rows.middle(1)
    row_gather = Gather(XR, xg, (xg.at[0, 0], xg.at[0, 1]))
    for h in (0, 1):
        rows.second[h].arrived()
        row_gather.to_right[h].start()
        row_gather.to_left[h].start()
    own_in.wait()
    own_out.wait()
    grad_rows.to_right[1].wait_recv()
    grad_rows.to_left[0].wait_recv()

    hidden_units = win.shape[0]
    step = 256

    def expert(d):
        def up(i, carry):
            at = pl.ds(pl.multiple_of(i * step, step), step)
            weight_in, weight_out = win[at, :], wout[at, :]
            signal = dot_nt(xg[d, 0], weight_in[:, :half]) + dot_nt(xg[d, 1], weight_in[:, half:])
            cotangent = dot_nt(gg[d, 0], weight_out[:, :half]) + dot_nt(gg[d, 1], weight_out[:, half:])
            square = signal * signal
            tangent = jnp.tanh(gelu_scale * (signal + cubic_weight * signal * square))
            upper = 0.5 * (1.0 + tangent)
            hid[:, at] = (signal * upper).astype(BF16)
            slope = upper + 0.5 * signal * (1.0 - tangent * tangent) * gelu_scale * (1.0 + 3.0 * cubic_weight * square)
            ghd[:, at] = (cotangent * slope).astype(BF16)
            return carry

        lax.fori_loop(0, hidden_units // step, up, 0)
        for n in range(width // step):
            at = slice(n * step, (n + 1) * step)
            h, low = divmod(n * step, half)
            inner = slice(low, low + step)
            part[0, d, h, :, inner] = dot_nn(ghd[...], win[:, at]).astype(BF16)
            part[1, d, h, :, inner] = dot_nn(hid[...], wout[:, at]).astype(BF16)

    sums = [Reduce(i, part.at[i], opp.at[i], near_l.at[i], near_r.at[i]) for i in (RG, RO)]
    expert(0)
    row_gather.forward_right()
    row_gather.forward_left()
    row_gather.to_right[1].wait_recv()
    expert(3)
    for total in sums:
        total.left_a.start()
    row_gather.to_left[0].wait_recv()
    expert(1)
    for total in sums:
        total.right_b.start()
    grad_rows.on_right.wait_recv()
    grad_rows.on_left.wait_recv()
    row_gather.on_right.wait_recv()
    row_gather.on_left.wait_recv()
    expert(2)
    for total in sums:
        total.opposite_a.start()
        total.opposite_b.start()
    for total in sums:
        total.pass_on()
    returns = []
    for i in (RG, RO):
        sums[i].arrived()
        back = Return((BG, BO)[i], 2 + i, back_x.at[i])
        for h in (0, 1):
            send[2 + i, h] = (
                part[i, 0, h].astype(F32) + near_l[i, h].astype(F32) + near_r[i, h].astype(F32)
            ).astype(BF16)
            back.first[h].start()
        returns.append(back)
    for back in returns:
        back.middle(0)
        back.middle(1)
    for back in returns:
        back.second[0].arrived()
        back.second[1].arrived()

    outs, grad_routed = [], None
    for j in (0, 1):
        outs.append(jnp.concatenate([dot_nn(pick[j], back_x[1, h]) for h in (0, 1)], axis=1))
        grad = gates[j] * jnp.concatenate([dot_nn(pick[j], back_x[0, h]) for h in (0, 1)], axis=1)
        grad_routed = grad if grad_routed is None else grad_routed + grad
    layer_ref[...] = (residual[...] + gates[0] * outs[0] + gates[1] * outs[1]).astype(BF16)
    cotangent = gout_ref[...].astype(F32)
    gate_grads = [jnp.sum(cotangent * out, axis=-1, keepdims=True) for out in outs]
    gate_mean = gates[0] * gate_grads[0] + gates[1] * gate_grads[1]
    parts = [gates[j] * (gate_grads[j] - gate_mean) for j in (0, 1)]
    rest = jnp.where(first_hot, parts[0], 0.0) + jnp.where(second_hot, parts[1], 0.0)
    for _ in range(3):
        piece = rest.astype(BF16)
        grad_routed = grad_routed + dot_nt(piece, router_ref[...])
        rest = rest - piece.astype(F32)
    grad_norm = grad_routed * gain_ref[...]
    state = normed[...]
    grad_states = cotangent + reciprocal * (
        grad_norm
        - jnp.mean(grad_norm, axis=-1, keepdims=True)
        - state * jnp.mean(grad_norm * state, axis=-1, keepdims=True)
    )
    gstates_ref[...] = grad_states.astype(BF16)

    def attend_back(head, carry):
        at = columns(head)
        key_rows = kvb[:, 0, :, at].reshape(sources, HD)
        value_rows = kvb[:, 1, :, at].reshape(sources, HD)
        probability = prob[head]
        grad_head = gstates_ref[:, at]
        grad_probability = dot_nt(grad_head, value_rows)
        inner = jnp.sum(probability * grad_probability, axis=-1, keepdims=True)
        grad_scores = (probability * (grad_probability - inner)).astype(BF16)
        gq_ref[:, at] = (dot_nn(grad_scores, key_rows) * score_scale).astype(BF16)
        key_part = (dot_tn(grad_scores, q_ref[:, at]) * score_scale).astype(BF16)
        value_part = dot_tn(probability.astype(BF16), grad_head).astype(BF16)
        kpart[:, 0, :, at] = key_part.reshape(ny, block_rows, HD)
        kpart[:, 1, :, at] = value_part.reshape(ny, block_rows, HD)
        return carry

    lax.fori_loop(0, H, attend_back, 0)
    key_sum = Reduce(RKV, kpart, kopp, knear_l, knear_r)
    key_sum.opposite_a.start()
    key_sum.opposite_b.start()
    key_sum.right_b.start()
    key_sum.left_a.start()
    key_sum.pass_on()
    key_sum.arrived()
    for h, out in ((0, gk_ref), (1, gv_ref)):
        out[...] = kpart[0, h].astype(F32) + knear_l[h].astype(F32) + knear_r[h].astype(F32)

    for gather in (keys, grad_rows, row_gather):
        gather.sent()
    for total in (*sums, key_sum):
        total.sent()
    for exchange in (grads, rows, *returns):
        exchange.sent()


def swap_matrix():
    at = np.arange(SLOTS)
    outer, middle, inner = at // GROUP, at % GROUP // CAP, at % CAP
    matrix = np.zeros((SLOTS, SLOTS), np.float32)
    matrix[at, middle * GROUP + outer * CAP + inner] = 1.0
    return matrix


def on_device(dec, q, k, v, lengths, gain, router, ids, win, wout, gout):
    tokens, width = dec.shape[1:]
    block_rows = k.shape[1]
    hidden_units = win.shape[1]
    half = width // 2
    vmem = pl.BlockSpec(memory_space=pltpu.VMEM)
    hbm = pl.BlockSpec(memory_space=pl.ANY)
    shape = jax.ShapeDtypeStruct
    rows = (2, SLOTS, half)
    outs = pl.pallas_call(
        layer,
        out_shape=(
            shape((tokens, width), BF16),
            shape((tokens, width), BF16),
            shape((tokens, width), BF16),
            shape((block_rows, width), F32),
            shape((block_rows, width), F32),
        ),
        in_specs=[
            pl.BlockSpec(memory_space=pltpu.SMEM),
            vmem,
            vmem,
            hbm,
            hbm,
            vmem,
            vmem,
            vmem,
            hbm,
            hbm,
            vmem,
            vmem,
        ],
        out_specs=[vmem] * 5,
        scratch_shapes=[
            pltpu.VMEM((4, 2, block_rows, width), BF16),
            pltpu.VMEM((hidden_units, width), BF16),
            pltpu.VMEM((hidden_units, width), BF16),
            pltpu.VMEM((4, *rows), BF16),
            pltpu.VMEM((4, *rows), BF16),
            pltpu.VMEM((4, *rows), BF16),
            pltpu.VMEM((4, *rows), BF16),
            pltpu.VMEM((4, *rows), BF16),
            pltpu.VMEM((2, tokens, SLOTS), BF16),
            pltpu.VMEM((H, tokens, 4 * block_rows), F32),
            pltpu.VMEM((tokens, width), F32),
            pltpu.VMEM((tokens, width), F32),
            pltpu.VMEM((SLOTS, hidden_units), BF16),
            pltpu.VMEM((SLOTS, hidden_units), BF16),
            pltpu.VMEM((2, 4, *rows), BF16),
            pltpu.VMEM((2, *rows), BF16),
            pltpu.VMEM((2, *rows), BF16),
            pltpu.VMEM((2, *rows), BF16),
            pltpu.VMEM((4, 2, block_rows, width), BF16),
            pltpu.VMEM((2, block_rows, width), BF16),
            pltpu.VMEM((2, block_rows, width), BF16),
            pltpu.VMEM((2, block_rows, width), BF16),
            pltpu.VMEM((2, *rows), BF16),
            pltpu.SemaphoreType.DMA((4,)),
            pltpu.SemaphoreType.DMA((18,)),
            pltpu.SemaphoreType.DMA((18,)),
            pltpu.SemaphoreType.DMA((18,)),
            pltpu.SemaphoreType.DMA((18,)),
            pltpu.SemaphoreType.DMA((16,)),
            pltpu.SemaphoreType.DMA((16,)),
        ],
        compiler_params=pltpu.CompilerParams(
            collective_id=0, has_side_effects=True, vmem_limit_bytes=62 * 2**20
        ),
        name="layer",
    )(
        lengths,
        dec[0],
        q[0],
        k[0],
        v[0],
        gain.reshape(1, width),
        router,
        ids[0],
        win[0],
        wout[0],
        gout[0],
        jnp.asarray(swap_matrix(), BF16),
    )
    return tuple(out[None] for out in outs)


def solution(mesh):
    rows = P("expert", "seq", None)
    return jax.shard_map(
        on_device,
        mesh=mesh,
        in_specs=(rows, rows, rows, rows, P("expert"), P(), P(), rows, rows, rows, rows),
        out_specs=(rows,) * 5,
        check_vma=False,
    )
```

```python
import functools
import math

import jax
import jax.numpy as jnp
import numpy as np
from jax import lax
from jax.experimental import pallas as pl
from jax.experimental.pallas import tpu as pltpu
from jax.sharding import PartitionSpec as P

H = 8
HD = 128
CAP = 6
SIDE = 8
GROUP = SIDE * CAP
SLOTS = SIDE * GROUP
MESH = pl.DeviceIdType.MESH
F32 = jnp.float32
BF16 = jnp.bfloat16

gelu_scale = 0.7978845608028654
cubic_weight = 0.044715

KV, GR, XR = 0, 1, 2
RG, RO, RKV = 0, 1, 2
AG, AX, BG, BO = 0, 1, 2, 3


def dot_nn(a, b):
    return lax.dot_general(a, b, (((1,), (0,)), ((), ())), preferred_element_type=F32)


def dot_nt(a, b):
    return lax.dot_general(a, b, (((1,), (1,)), ((), ())), preferred_element_type=F32)


def dot_tn(a, b):
    return lax.dot_general(a, b, (((0,), (0,)), ((), ())), preferred_element_type=F32)


def layer(
    length_ref,
    dec_ref,
    q_ref,
    k_ref,
    v_ref,
    gain_ref,
    router_ref,
    ids_ref,
    win_ref,
    wout_ref,
    gout_ref,
    swap_ref,
    layer_ref,
    gstates_ref,
    gq_ref,
    gk_ref,
    gv_ref,
    kvb,
    win,
    wout,
    xg,
    gg,
    send,
    zbuf,
    turned,
    pick,
    prob,
    residual,
    normed,
    hid,
    ghd,
    part,
    opp,
    near_l,
    near_r,
    kpart,
    kopp,
    knear_l,
    knear_r,
    back_x,
    slopes,
    gate_part,
    gate_near,
    gate_rows,
    local_sem,
    ag_s,
    ag_r,
    rs_s,
    rs_r,
    xs_s,
    xs_r,
    gate_s,
    gate_r,
):
    tokens, width = dec_ref.shape
    half = width // 2
    ny = lax.axis_size("seq")
    y = lax.axis_index("seq")
    e = lax.axis_index("expert")
    core = lax.rem(e, 2)
    z = lax.rem(e // 2, SIDE)
    x = e // (2 * SIDE)
    xc = x * 2 + core
    right = (lax.rem(y + 1, ny), e)
    left = (lax.rem(y + ny - 1, ny), e)
    across = (lax.rem(y + 2, ny), e)
    hops = (4, 3, 5, 2, 6, 1, 7)

    def z_peer(hop):
        there = lax.rem(z + hop, SIDE)
        return there, (y, x * (2 * SIDE) + there * 2 + core)

    def xc_peer(hop):
        there = lax.rem(xc + hop, SIDE)
        return there, (y, (there // 2) * (2 * SIDE) + z * 2 + lax.rem(there, 2))

    def remote(src, dst, s, r, device):
        return pltpu.make_async_remote_copy(
            src_ref=src, dst_ref=dst, send_sem=s, recv_sem=r, device_id=device, device_id_type=MESH
        )

    own_k = pltpu.make_async_copy(k_ref, kvb.at[0, 0], local_sem.at[0])
    own_v = pltpu.make_async_copy(v_ref, kvb.at[0, 1], local_sem.at[1])
    own_in = pltpu.make_async_copy(win_ref, win, local_sem.at[2])
    own_out = pltpu.make_async_copy(wout_ref, wout, local_sem.at[3])
    for copy in (own_k, own_v, own_in, own_out):
        copy.start()

    barrier = pltpu.get_barrier_semaphore()
    for device in (left, right, across):
        pl.semaphore_signal(barrier, inc=1, device_id=device, device_id_type=MESH)
    for hop in hops:
        pl.semaphore_signal(barrier, inc=1, device_id=z_peer(hop)[1], device_id_type=MESH)
        pl.semaphore_signal(barrier, inc=1, device_id=xc_peer(hop)[1], device_id_type=MESH)

    class Gather:
        def __init__(self, number, buf, sources):
            def at(i):
                return ag_s.at[number * 6 + i], ag_r.at[number * 6 + i]

            self.to_right = [remote(sources[h], buf.at[3, h], *at(h), right) for h in (0, 1)]
            self.to_left = [remote(sources[h], buf.at[1, h], *at(2 + h), left) for h in (0, 1)]
            self.on_right = remote(buf.at[3, 0], buf.at[2, 0], *at(4), right)
            self.on_left = remote(buf.at[1, 1], buf.at[2, 1], *at(5), left)

        def forward_right(self):
            self.to_right[0].wait_recv()
            self.on_right.start()

        def forward_left(self):
            self.to_left[1].wait_recv()
            self.on_left.start()

        def sent(self):
            for copy in (*self.to_right, *self.to_left, self.on_right, self.on_left):
                copy.wait_send()

    class Reduce:
        def __init__(self, number, parts, crossed, from_left, from_right):
            def at(i):
                return rs_s.at[number * 6 + i], rs_r.at[number * 6 + i]

            self.parts, self.crossed = parts, crossed
            self.left_a = remote(parts.at[3, 0], from_right.at[0], *at(0), left)
            self.right_b = remote(parts.at[1, 1], from_left.at[1], *at(1), right)
            self.opposite_a = remote(parts.at[2, 0], crossed.at[0], *at(2), right)
            self.opposite_b = remote(parts.at[2, 1], crossed.at[1], *at(3), left)
            self.right_a = remote(parts.at[1, 0], from_left.at[0], *at(4), right)
            self.left_b = remote(parts.at[3, 1], from_right.at[1], *at(5), left)

        def pass_on(self):
            self.opposite_a.wait_recv()
            self.parts[1, 0] = (self.parts[1, 0].astype(F32) + self.crossed[0].astype(F32)).astype(BF16)
            self.right_a.start()
            self.opposite_b.wait_recv()
            self.parts[3, 1] = (self.parts[3, 1].astype(F32) + self.crossed[1].astype(F32)).astype(BF16)
            self.left_b.start()

        def arrived(self):
            for copy in (self.left_a, self.right_b, self.right_a, self.left_b):
                copy.wait_recv()

        def sent(self):
            for copy in (self.left_a, self.right_b, self.opposite_a, self.opposite_b, self.right_a, self.left_b):
                copy.wait_send()

    class Stage:
        def __init__(self, number, src, dst, peer, mine):
            self.s, self.r = xs_s.at[number], xs_r.at[number]
            self.src, self.dst, self.peer, self.mine = src, dst, peer, mine

        def rows(self, at):
            return pl.ds(pl.multiple_of(at * GROUP, 16), GROUP)

        def start(self):
            own = self.rows(self.mine)
            for hop in hops:
                there, device = self.peer(hop)
                remote(self.src.at[self.rows(there)], self.dst.at[own], self.s, self.r, device).start()
            pltpu.make_async_copy(self.src.at[own], self.dst.at[own], self.r).start()

        def arrived(self):
            pltpu.make_async_copy(self.src, self.dst, self.r).wait()

        def sent(self):
            most = pl.ds(0, SLOTS - GROUP)
            remote(self.src.at[most], self.dst.at[most], self.s, self.r, right).wait_send()

    def turn(src, dst):
        dst[...] = dot_nn(swap_ref[...], src[...]).astype(BF16)

    class Dispatch:
        def __init__(self, number, tensor, dst):
            self.first = [Stage(number * 4 + h, send.at[tensor, h], zbuf.at[tensor, h], z_peer, z) for h in (0, 1)]
            self.second = [Stage(number * 4 + 2 + h, turned.at[tensor, h], dst.at[h], xc_peer, xc) for h in (0, 1)]
            self.tensor = tensor

        def middle(self, h):
            self.first[h].arrived()
            turn(zbuf.at[self.tensor, h], turned.at[self.tensor, h])
            self.second[h].start()

        def sent(self):
            for stage in (*self.first, *self.second):
                stage.sent()

    class Return:
        def __init__(self, number, tensor, dst):
            self.first = [Stage(number * 4 + h, send.at[tensor, h], zbuf.at[tensor, h], xc_peer, xc) for h in (0, 1)]
            self.second = [Stage(number * 4 + 2 + h, turned.at[tensor, h], dst.at[h], z_peer, z) for h in (0, 1)]
            self.tensor = tensor

        middle = Dispatch.middle
        sent = Dispatch.sent

    experts = router_ref.shape[0]
    named = [
        jnp.broadcast_to(ids_ref[j : j + 1, :].astype(F32), (tokens, tokens)).T[:, :experts].astype(jnp.int32)
        for j in (0, 1)
    ]
    lanes = lax.broadcasted_iota(jnp.int32, (tokens, experts), 1)
    first_hot = named[0] == lanes
    second_hot = named[1] == lanes
    ones = first_hot.astype(F32), second_hot.astype(F32)
    earlier = (
        lax.broadcasted_iota(jnp.int32, (tokens, tokens), 0) > lax.broadcasted_iota(jnp.int32, (tokens, tokens), 1)
    ).astype(F32).astype(BF16)
    slot_lanes = lax.broadcasted_iota(jnp.int32, (tokens, SLOTS), 1)
    base = ((lanes // 2) % SIDE) * GROUP + (lanes // (2 * SIDE)) * (2 * CAP) + (lanes % 2) * CAP
    both = jnp.zeros((tokens, SLOTS), F32)
    for j in (0, 1):
        rank = dot_nn(earlier, ones[j].astype(BF16))
        if j == 1:
            rank = rank + jnp.sum(ones[0], axis=0, keepdims=True)
        slot = jnp.sum(ones[j] * (rank + base.astype(F32)), axis=-1, keepdims=True)
        chosen = (slot.astype(jnp.int32) == slot_lanes).astype(F32)
        pick[j] = chosen.astype(BF16)
        both = both + chosen
    spread = both.T.astype(BF16)
    for h in (0, 1):
        send[0, h] = dot_nn(spread, gout_ref[:, h * half : (h + 1) * half]).astype(BF16)

    pl.semaphore_wait(barrier, 3 + 2 * len(hops))
    keys = Gather(KV, kvb, (k_ref, v_ref))
    grads = Dispatch(AG, 0, gg.at[0])
    keys.to_right[0].start()
    keys.to_left[1].start()
    grads.first[0].start()
    keys.to_right[1].start()
    keys.to_left[0].start()
    grads.first[1].start()
    keys.forward_right()
    keys.forward_left()
    grads.middle(0)
    grads.middle(1)
    keys.to_right[1].wait_recv()
    keys.to_left[0].wait_recv()
    own_k.wait()
    own_v.wait()
    keys.on_right.wait_recv()
    keys.on_left.wait_recv()

    score_scale = 1.0 / math.sqrt(HD)
    block_rows = kvb.shape[2]
    sources = ny * block_rows
    place = lax.broadcasted_iota(jnp.int32, (tokens, sources), 1)
    place = (place // block_rows + y) % ny * block_rows + place % block_rows
    valid = place < length_ref[0]

    def columns(head):
        return pl.ds(pl.multiple_of(head * HD, HD), HD)

    def attend(head, carry):
        at = columns(head)
        key_rows = kvb[:, 0, :, at].reshape(sources, HD)
        scores = dot_nt(q_ref[:, at], key_rows) * score_scale
        scores = jnp.where(valid, scores, -1e30)
        raw = jnp.exp(scores - jnp.max(scores, axis=-1, keepdims=True))
        probability = raw / jnp.sum(raw, axis=-1, keepdims=True)
        prob[head] = probability
        value_rows = kvb[:, 1, :, at].reshape(sources, HD)
        residual[:, at] = dec_ref[:, at].astype(F32) + dot_nn(probability.astype(BF16), value_rows)
        return carry

    grad_rows = Gather(GR, gg, (gg.at[0, 0], gg.at[0, 1]))
    for h in (0, 1):
        grads.second[h].arrived()
        grad_rows.to_right[h].start()
        grad_rows.to_left[h].start()
        lax.fori_loop(h * (H // 2), (h + 1) * (H // 2), attend, 0)

    whole = residual[...]
    centred = whole - jnp.mean(whole, axis=-1, keepdims=True)
    reciprocal = 1.0 / jnp.sqrt(jnp.mean(centred * centred, axis=-1, keepdims=True) + 1e-05)
    normed[...] = centred * reciprocal
    routed_in = (normed[...] * gain_ref[...]).astype(BF16)
    for h in (0, 1):
        send[1, h] = dot_nn(spread, routed_in[:, h * half : (h + 1) * half]).astype(BF16)
    rows = Dispatch(AX, 1, xg.at[0])
    rows.first[0].start()
    rows.first[1].start()

    logits = dot_nt(routed_in, router_ref[...])
    first_logit = jnp.sum(jnp.where(first_hot, logits, 0.0), axis=-1, keepdims=True)
    second_logit = jnp.sum(jnp.where(second_hot, logits, 0.0), axis=-1, keepdims=True)
    gates = 1.0 / (1.0 + jnp.exp(second_logit - first_logit)), 1.0 / (1.0 + jnp.exp(first_logit - second_logit))

    grad_rows.forward_right()
    rows.middle(0)
    grad_rows.forward_left()
    rows.middle(1)
    row_gather = Gather(XR, xg, (xg.at[0, 0], xg.at[0, 1]))
    for h in (0, 1):
        rows.second[h].arrived()
        row_gather.to_right[h].start()
        row_gather.to_left[h].start()
    own_in.wait()
    own_out.wait()
    grad_rows.to_right[1].wait_recv()
    grad_rows.to_left[0].wait_recv()

    hidden_units = win.shape[0]
    step = 256

    def expert(d):
        def up(i, carry):
            at = pl.ds(pl.multiple_of(i * step, step), step)
            weight_in, weight_out = win[at, :], wout[at, :]
            signal = dot_nt(xg[d, 0], weight_in[:, :half]) + dot_nt(xg[d, 1], weight_in[:, half:])
            cotangent = dot_nt(gg[d, 0], weight_out[:, :half]) + dot_nt(gg[d, 1], weight_out[:, half:])
            square = signal * signal
            tangent = jnp.tanh(gelu_scale * (signal + cubic_weight * signal * square))
            upper = 0.5 * (1.0 + tangent)
            hid[:, at] = (signal * upper).astype(BF16)
            slope = upper + 0.5 * signal * (1.0 - tangent * tangent) * gelu_scale * (1.0 + 3.0 * cubic_weight * square)
            ghd[:, at] = (cotangent * slope).astype(BF16)
            return carry

        lax.fori_loop(0, hidden_units // step, up, 0)
        gate = jnp.zeros((SLOTS, 1), F32)
        for n in range(width // step):
            at = slice(n * step, (n + 1) * step)
            h, low = divmod(n * step, half)
            inner = slice(low, low + step)
            part[0, d, h, :, inner] = dot_nn(ghd[...], win[:, at]).astype(BF16)
            result = dot_nn(hid[...], wout[:, at])
            gate = gate + jnp.sum(result * gg[d, h, :, inner].astype(F32), axis=-1, keepdims=True)
            part[1, d, h, :, inner] = result.astype(BF16)
        gate_part[d] = jnp.broadcast_to(gate, (SLOTS, HD)).T[:8]

    sums = [Reduce(i, part.at[i], opp.at[i], near_l.at[i], near_r.at[i]) for i in (RG, RO)]
    gate_sums = [
        remote(gate_part.at[d], gate_near.at[d - 1], gate_s.at[d - 1], gate_r.at[d - 1], device)
        for d, device in ((1, right), (2, across), (3, left))
    ]
    expert(0)
    row_gather.forward_right()
    row_gather.forward_left()
    row_gather.to_right[1].wait_recv()
    expert(3)
    gate_sums[2].start()
    sums[RG].left_a.start()
    row_gather.to_left[0].wait_recv()
    expert(1)
    gate_sums[0].start()
    sums[RG].right_b.start()
    grad_rows.on_right.wait_recv()
    grad_rows.on_left.wait_recv()
    row_gather.on_right.wait_recv()
    row_gather.on_left.wait_recv()
    expert(2)
    gate_sums[1].start()
    sums[RG].opposite_a.start()
    sums[RG].opposite_b.start()
    sums[RG].pass_on()
    for copy in (sums[RO].opposite_a, sums[RO].opposite_b, sums[RO].right_b, sums[RO].left_a):
        copy.start()

    for copy in gate_sums:
        copy.wait_recv()
    gate_total = gate_part[0] + gate_near[0] + gate_near[1] + gate_near[2]
    rest = jnp.broadcast_to(gate_total[0:1], (HD, SLOTS)).T
    piece_lanes = lax.broadcasted_iota(jnp.int32, (SLOTS, HD), 1)
    packed = jnp.zeros((SLOTS, HD), F32)
    for n in range(3):
        piece = rest.astype(BF16).astype(F32)
        packed = packed + jnp.where(piece_lanes == n, piece, 0.0)
        rest = rest - piece
    gate_rows[0] = packed.astype(BF16)
    gate_first = Stage(16, gate_rows.at[0], gate_rows.at[1], xc_peer, xc)
    gate_second = Stage(17, gate_rows.at[2], gate_rows.at[3], z_peer, z)
    gate_first.start()

    def send_back(i):
        back = Return((BG, BO)[i], 2 + i, back_x.at[i])
        for h in (0, 1):
            send[2 + i, h] = (
                part[i, 0, h].astype(F32) + near_l[i, h].astype(F32) + near_r[i, h].astype(F32)
            ).astype(BF16)
            back.first[h].start()
        return back

    sums[RG].arrived()
    grads_back = send_back(RG)
    gate_first.arrived()
    turn(gate_rows.at[1], gate_rows.at[2])
    gate_second.start()
    grads_back.middle(0)
    grads_back.middle(1)
    sums[RO].pass_on()
    gate_second.arrived()
    grads_back.second[0].arrived()
    grads_back.second[1].arrived()

    cotangent = gout_ref[...].astype(F32)
    grad_routed, gate_grads = None, []
    for j in (0, 1):
        grad = gates[j] * jnp.concatenate([dot_nn(pick[j], back_x[RG, h]) for h in (0, 1)], axis=1)
        grad_routed = grad if grad_routed is None else grad_routed + grad
        gate_grads.append(jnp.sum(dot_nn(pick[j], gate_rows[3]), axis=-1, keepdims=True))
    gate_mean = gates[0] * gate_grads[0] + gates[1] * gate_grads[1]
    parts = [gates[j] * (gate_grads[j] - gate_mean) for j in (0, 1)]
    rest = jnp.where(first_hot, parts[0], 0.0) + jnp.where(second_hot, parts[1], 0.0)
    for _ in range(3):
        piece = rest.astype(BF16)
        grad_routed = grad_routed + dot_nn(piece, router_ref[...])
        rest = rest - piece.astype(F32)
    grad_norm = grad_routed * gain_ref[...]
    state = normed[...]
    grad_states = cotangent + reciprocal * (
        grad_norm
        - jnp.mean(grad_norm, axis=-1, keepdims=True)
        - state * jnp.mean(grad_norm * state, axis=-1, keepdims=True)
    )
    gstates_ref[...] = grad_states.astype(BF16)

    def value_grads(head, carry):
        at = columns(head)
        rows_of = dot_tn(prob[head].astype(BF16), gstates_ref[:, at]).astype(BF16)
        kpart[:, 1, :, at] = rows_of.reshape(ny, block_rows, HD)
        return carry

    def key_grads(head, carry):
        at = columns(head)
        value_rows = kvb[:, 1, :, at].reshape(sources, HD)
        probability = prob[head]
        grad_probability = dot_nt(gstates_ref[:, at], value_rows)
        inner = jnp.sum(probability * grad_probability, axis=-1, keepdims=True)
        grad_scores = (probability * (grad_probability - inner)).astype(BF16)
        slopes[head] = grad_scores
        rows_of = (dot_tn(grad_scores, q_ref[:, at]) * score_scale).astype(BF16)
        kpart[:, 0, :, at] = rows_of.reshape(ny, block_rows, HD)
        return carry

    def query_grads(head, carry):
        at = columns(head)
        key_rows = kvb[:, 0, :, at].reshape(sources, HD)
        gq_ref[:, at] = (dot_nn(slopes[head], key_rows) * score_scale).astype(BF16)
        return carry

    key_sum = Reduce(RKV, kpart, kopp, knear_l, knear_r)
    lax.fori_loop(0, H, value_grads, 0)
    key_sum.opposite_b.start()
    key_sum.right_b.start()
    lax.fori_loop(0, H, key_grads, 0)
    key_sum.opposite_a.start()
    key_sum.left_a.start()
    sums[RO].arrived()
    outs_back = send_back(RO)
    lax.fori_loop(0, H, query_grads, 0)
    outs_back.middle(0)
    outs_back.middle(1)
    key_sum.pass_on()
    outs_back.second[0].arrived()
    outs_back.second[1].arrived()
    outs = [jnp.concatenate([dot_nn(pick[j], back_x[RO, h]) for h in (0, 1)], axis=1) for j in (0, 1)]
    layer_ref[...] = (residual[...] + gates[0] * outs[0] + gates[1] * outs[1]).astype(BF16)
    key_sum.arrived()
    for h, out in ((0, gk_ref), (1, gv_ref)):
        out[...] = kpart[0, h].astype(F32) + knear_l[h].astype(F32) + knear_r[h].astype(F32)

    for gather in (keys, grad_rows, row_gather):
        gather.sent()
    for total in (*sums, key_sum):
        total.sent()
    for exchange in (grads, rows, grads_back, outs_back, gate_first, gate_second):
        exchange.sent()
    for copy in gate_sums:
        copy.wait_send()


def hand_over(*refs):
    *refs, sems = refs
    count = len(refs) // 2
    copies = [pltpu.make_async_copy(refs[i], refs[count + i], sems.at[i]) for i in range(count)]
    for copy in copies:
        copy.start()
    for copy in copies:
        copy.wait()


def swap_matrix():
    at = np.arange(SLOTS)
    outer, middle, inner = at // GROUP, at % GROUP // CAP, at % CAP
    matrix = np.zeros((SLOTS, SLOTS), np.float32)
    matrix[at, middle * GROUP + outer * CAP + inner] = 1.0
    return matrix


def on_device(dec, q, k, v, lengths, gain, router, ids, win, wout, gout):
    tokens, width = dec.shape[1:]
    block_rows = k.shape[1]
    hidden_units = win.shape[1]
    half = width // 2
    vmem = pl.BlockSpec(memory_space=pltpu.VMEM)
    hbm = pl.BlockSpec(memory_space=pl.ANY)
    shape = jax.ShapeDtypeStruct
    rows = (2, SLOTS, half)
    outs = pl.pallas_call(
        layer,
        out_shape=(
            shape((tokens, width), BF16),
            shape((tokens, width), BF16),
            shape((tokens, width), BF16),
            shape((block_rows, width), F32),
            shape((block_rows, width), F32),
        ),
        in_specs=[
            pl.BlockSpec(memory_space=pltpu.SMEM),
            vmem,
            vmem,
            hbm,
            hbm,
            vmem,
            vmem,
            vmem,
            hbm,
            hbm,
            vmem,
            vmem,
        ],
        out_specs=[vmem] * 5,
        scratch_shapes=[
            pltpu.VMEM((4, 2, block_rows, width), BF16),
            pltpu.VMEM((hidden_units, width), BF16),
            pltpu.VMEM((hidden_units, width), BF16),
            pltpu.VMEM((4, *rows), BF16),
            pltpu.VMEM((4, *rows), BF16),
            pltpu.VMEM((4, *rows), BF16),
            pltpu.VMEM((4, *rows), BF16),
            pltpu.VMEM((4, *rows), BF16),
            pltpu.VMEM((2, tokens, SLOTS), BF16),
            pltpu.VMEM((H, tokens, 4 * block_rows), F32),
            pltpu.VMEM((tokens, width), F32),
            pltpu.VMEM((tokens, width), F32),
            pltpu.VMEM((SLOTS, hidden_units), BF16),
            pltpu.VMEM((SLOTS, hidden_units), BF16),
            pltpu.VMEM((2, 4, *rows), BF16),
            pltpu.VMEM((2, *rows), BF16),
            pltpu.VMEM((2, *rows), BF16),
            pltpu.VMEM((2, *rows), BF16),
            pltpu.VMEM((4, 2, block_rows, width), BF16),
            pltpu.VMEM((2, block_rows, width), BF16),
            pltpu.VMEM((2, block_rows, width), BF16),
            pltpu.VMEM((2, block_rows, width), BF16),
            pltpu.VMEM((2, *rows), BF16),
            pltpu.VMEM((H, tokens, 4 * block_rows), BF16),
            pltpu.VMEM((4, 8, SLOTS), F32),
            pltpu.VMEM((3, 8, SLOTS), F32),
            pltpu.VMEM((4, SLOTS, HD), BF16),
            pltpu.SemaphoreType.DMA((4,)),
            pltpu.SemaphoreType.DMA((18,)),
            pltpu.SemaphoreType.DMA((18,)),
            pltpu.SemaphoreType.DMA((18,)),
            pltpu.SemaphoreType.DMA((18,)),
            pltpu.SemaphoreType.DMA((18,)),
            pltpu.SemaphoreType.DMA((18,)),
            pltpu.SemaphoreType.DMA((3,)),
            pltpu.SemaphoreType.DMA((3,)),
        ],
        compiler_params=pltpu.CompilerParams(
            collective_id=0, has_side_effects=True, vmem_limit_bytes=62 * 2**20
        ),
        name="layer",
    )(
        lengths,
        dec[0],
        q[0],
        k[0],
        v[0],
        gain.reshape(1, width),
        router.T,
        ids[0].T,
        win[0],
        wout[0],
        gout[0],
        jnp.asarray(swap_matrix(), BF16),
    )
    count = len(outs)
    outs = pl.pallas_call(
        hand_over,
        out_shape=tuple(shape(out.shape, out.dtype) for out in outs),
        in_specs=[hbm] * count,
        out_specs=[hbm] * count,
        scratch_shapes=[pltpu.SemaphoreType.DMA((count,))],
        name="hand_over",
    )(*outs)
    return tuple(out[None] for out in outs)


def solution(mesh):
    rows = P("expert", "seq", None)
    return jax.shard_map(
        on_device,
        mesh=mesh,
        in_specs=(rows, rows, rows, rows, P("expert"), P(), P(), rows, rows, rows, rows),
        out_specs=(rows,) * 5,
        check_vma=False,
    )
```

```python
import functools
import math

import jax
import jax.numpy as jnp
import numpy as np
from jax import lax
from jax.experimental import pallas as pl
from jax.experimental.pallas import tpu as pltpu
from jax.sharding import PartitionSpec as P

H = 8
HD = 128
CAP = 6
SIDE = 8
GROUP = SIDE * CAP
SLOTS = SIDE * GROUP
MESH = pl.DeviceIdType.MESH
F32 = jnp.float32
BF16 = jnp.bfloat16

gelu_scale = 0.7978845608028654
cubic_weight = 0.044715

KV, GR, XR = 0, 1, 2
RG, RO, RKV = 0, 1, 2
AG, AX, BG, BO = 0, 1, 2, 3


def dot_nn(a, b):
    return lax.dot_general(a, b, (((1,), (0,)), ((), ())), preferred_element_type=F32)


def dot_nt(a, b):
    return lax.dot_general(a, b, (((1,), (1,)), ((), ())), preferred_element_type=F32)


def dot_tn(a, b):
    return lax.dot_general(a, b, (((0,), (0,)), ((), ())), preferred_element_type=F32)


def layer(
    length_ref,
    dec_ref,
    q_ref,
    k_ref,
    v_ref,
    gain_ref,
    router_ref,
    ids_ref,
    win_ref,
    wout_ref,
    gout_ref,
    swap_ref,
    layer_ref,
    gstates_ref,
    gq_ref,
    gk_ref,
    gv_ref,
    kvb,
    win,
    wout,
    xg,
    gg,
    send,
    zbuf,
    turned,
    pick,
    prob,
    residual,
    normed,
    hid,
    ghd,
    part,
    opp,
    near_l,
    near_r,
    kpart,
    kopp,
    knear_l,
    knear_r,
    back_x,
    slopes,
    gate_part,
    gate_near,
    gate_rows,
    landed,
    ready,
    local_sem,
    ag_s,
    ag_r,
    rs_s,
    rs_r,
    xs_s,
    xs_r,
    gate_s,
    gate_r,
):
    tokens, width = dec_ref.shape
    half = width // 2
    ny = lax.axis_size("seq")
    y = lax.axis_index("seq")
    e = lax.axis_index("expert")
    core = lax.rem(e, 2)
    z = lax.rem(e // 2, SIDE)
    x = e // (2 * SIDE)
    xc = x * 2 + core
    right = (lax.rem(y + 1, ny), e)
    left = (lax.rem(y + ny - 1, ny), e)
    across = (lax.rem(y + 2, ny), e)
    hops = (4, 3, 5, 2, 6, 1, 7)

    def z_peer(hop):
        there = lax.rem(z + hop, SIDE)
        return there, (y, x * (2 * SIDE) + there * 2 + core)

    def xc_peer(hop):
        there = lax.rem(xc + hop, SIDE)
        return there, (y, (there // 2) * (2 * SIDE) + z * 2 + lax.rem(there, 2))

    def remote(src, dst, s, r, device):
        return pltpu.make_async_remote_copy(
            src_ref=src, dst_ref=dst, send_sem=s, recv_sem=r, device_id=device, device_id_type=MESH
        )

    own_k = pltpu.make_async_copy(k_ref, kvb.at[0, 0], local_sem.at[0])
    own_v = pltpu.make_async_copy(v_ref, kvb.at[0, 1], local_sem.at[1])
    own_in = pltpu.make_async_copy(win_ref, win, local_sem.at[2])
    own_out = pltpu.make_async_copy(wout_ref, wout, local_sem.at[3])
    for copy in (own_k, own_v, own_in, own_out):
        copy.start()

    barrier = pltpu.get_barrier_semaphore()
    for device in (left, right, across):
        pl.semaphore_signal(barrier, inc=1, device_id=device, device_id_type=MESH)
    for hop in hops:
        pl.semaphore_signal(barrier, inc=1, device_id=z_peer(hop)[1], device_id_type=MESH)
        pl.semaphore_signal(barrier, inc=1, device_id=xc_peer(hop)[1], device_id_type=MESH)

    class Gather:
        def __init__(self, number, buf, sources):
            def at(i):
                return ag_s.at[number * 6 + i], ag_r.at[number * 6 + i]

            self.to_right = [remote(sources[h], buf.at[3, h], *at(h), right) for h in (0, 1)]
            self.to_left = [remote(sources[h], buf.at[1, h], *at(2 + h), left) for h in (0, 1)]
            self.on_right = remote(buf.at[3, 0], buf.at[2, 0], *at(4), right)
            self.on_left = remote(buf.at[1, 1], buf.at[2, 1], *at(5), left)

        def forward_right(self):
            self.to_right[0].wait_recv()
            self.on_right.start()

        def forward_left(self):
            self.to_left[1].wait_recv()
            self.on_left.start()

        def sent(self):
            for copy in (*self.to_right, *self.to_left, self.on_right, self.on_left):
                copy.wait_send()

    class Reduce:
        def __init__(self, number, parts, crossed, from_left, from_right):
            def at(i):
                return rs_s.at[number * 6 + i], rs_r.at[number * 6 + i]

            self.parts, self.crossed = parts, crossed
            self.left_a = remote(parts.at[3, 0], from_right.at[0], *at(0), left)
            self.right_b = remote(parts.at[1, 1], from_left.at[1], *at(1), right)
            self.opposite_a = remote(parts.at[2, 0], crossed.at[0], *at(2), right)
            self.opposite_b = remote(parts.at[2, 1], crossed.at[1], *at(3), left)
            self.right_a = remote(parts.at[1, 0], from_left.at[0], *at(4), right)
            self.left_b = remote(parts.at[3, 1], from_right.at[1], *at(5), left)

        def pass_a(self):
            self.opposite_a.wait_recv()
            self.parts[1, 0] = (self.parts[1, 0].astype(F32) + self.crossed[0].astype(F32)).astype(BF16)
            self.right_a.start()

        def pass_b(self):
            self.opposite_b.wait_recv()
            self.parts[3, 1] = (self.parts[3, 1].astype(F32) + self.crossed[1].astype(F32)).astype(BF16)
            self.left_b.start()

        def pass_on(self):
            self.pass_a()
            self.pass_b()

        def arrived(self):
            for copy in (self.left_a, self.right_b, self.right_a, self.left_b):
                copy.wait_recv()

        def sent(self):
            for copy in (self.left_a, self.right_b, self.opposite_a, self.opposite_b, self.right_a, self.left_b):
                copy.wait_send()

    class Stage:
        def __init__(self, number, src, dst, peer, mine):
            self.s, self.r = xs_s.at[number], xs_r.at[number]
            self.src, self.dst, self.peer, self.mine = src, dst, peer, mine

        def rows(self, at):
            return pl.ds(pl.multiple_of(at * GROUP, 16), GROUP)

        def start(self):
            own = self.rows(self.mine)
            for hop in hops:
                there, device = self.peer(hop)
                remote(self.src.at[self.rows(there)], self.dst.at[own], self.s, self.r, device).start()
            pltpu.make_async_copy(self.src.at[own], self.dst.at[own], self.r).start()

        def arrived(self):
            pltpu.make_async_copy(self.src, self.dst, self.r).wait()

        def sent(self):
            most = pl.ds(0, SLOTS - GROUP)
            remote(self.src.at[most], self.dst.at[most], self.s, self.r, right).wait_send()

    def turn(src, dst):
        dst[...] = dot_nn(swap_ref[...], src[...]).astype(BF16)

    class Exchange:
        def __init__(self, number, tensor, dst, stages):
            here = (send, zbuf, turned)
            self.first, self.second, self.tensor, self.dst = [], [], tensor, dst
            for h in (0, 1):
                leave, between, go_on = (buf.at[tensor, h] for buf in here)
                end = dst.at[0] if h == 0 else landed.at[tensor]
                one, two = stages if h == 0 else stages[::-1]
                self.first.append(Stage(number * 4 + h, leave, between, *one))
                self.second.append(Stage(number * 4 + 2 + h, go_on, end, *two))

        def middle(self, h):
            self.first[h].arrived()
            turn(zbuf.at[self.tensor, h], turned.at[self.tensor, h])
            self.second[h].start()

        def finish(self, h):
            self.second[h].arrived()
            if h == 1:
                turn(landed.at[self.tensor], self.dst.at[1])

        def sent(self):
            for stage in (*self.first, *self.second):
                stage.sent()

    along_z, along_xc = (z_peer, z), (xc_peer, xc)

    experts = router_ref.shape[0]
    named = [
        jnp.broadcast_to(ids_ref[j : j + 1, :].astype(F32), (tokens, tokens)).T[:, :experts].astype(jnp.int32)
        for j in (0, 1)
    ]
    lanes = lax.broadcasted_iota(jnp.int32, (tokens, experts), 1)
    first_hot = named[0] == lanes
    second_hot = named[1] == lanes
    ones = first_hot.astype(F32), second_hot.astype(F32)
    earlier = (
        lax.broadcasted_iota(jnp.int32, (tokens, tokens), 0) > lax.broadcasted_iota(jnp.int32, (tokens, tokens), 1)
    ).astype(F32).astype(BF16)
    slot_lanes = lax.broadcasted_iota(jnp.int32, (tokens, SLOTS), 1)
    base = ((lanes // 2) % SIDE) * GROUP + (lanes // (2 * SIDE)) * (2 * CAP) + (lanes % 2) * CAP
    both = jnp.zeros((tokens, SLOTS), F32)
    for j in (0, 1):
        rank = dot_nn(earlier, ones[j].astype(BF16))
        if j == 1:
            rank = rank + jnp.sum(ones[0], axis=0, keepdims=True)
        slot = jnp.sum(ones[j] * (rank + base.astype(F32)), axis=-1, keepdims=True)
        chosen = (slot.astype(jnp.int32) == slot_lanes).astype(F32)
        pick[j] = chosen.astype(BF16)
        both = both + chosen
    spread = [both.T.astype(BF16)]
    spread.append(dot_nn(swap_ref[...], spread[0]).astype(BF16))
    for h in (0, 1):
        send[0, h] = dot_nn(spread[h], gout_ref[:, h * half : (h + 1) * half]).astype(BF16)

    pl.semaphore_wait(barrier, 3 + 2 * len(hops))
    keys = Gather(KV, kvb, (k_ref, v_ref))
    grads = Exchange(AG, 0, gg.at[0], (along_z, along_xc))
    keys.to_right[0].start()
    keys.to_left[1].start()
    grads.first[0].start()
    keys.to_right[1].start()
    keys.to_left[0].start()
    grads.first[1].start()
    keys.forward_right()
    keys.forward_left()
    grads.middle(1)
    grads.middle(0)
    keys.to_right[1].wait_recv()
    keys.to_left[0].wait_recv()
    own_k.wait()
    own_v.wait()
    keys.on_right.wait_recv()
    keys.on_left.wait_recv()

    score_scale = 1.0 / math.sqrt(HD)
    block_rows = kvb.shape[2]
    sources = ny * block_rows
    place = lax.broadcasted_iota(jnp.int32, (tokens, sources), 1)
    place = (place // block_rows + y) % ny * block_rows + place % block_rows
    valid = place < length_ref[0]

    def columns(head):
        return pl.ds(pl.multiple_of(head * HD, HD), HD)

    def attend(head, carry):
        at = columns(head)
        key_rows = kvb[:, 0, :, at].reshape(sources, HD)
        scores = dot_nt(q_ref[:, at], key_rows) * score_scale
        scores = jnp.where(valid, scores, -1e30)
        raw = jnp.exp(scores - jnp.max(scores, axis=-1, keepdims=True))
        probability = raw / jnp.sum(raw, axis=-1, keepdims=True)
        prob[head] = probability
        value_rows = kvb[:, 1, :, at].reshape(sources, HD)
        residual[:, at] = dec_ref[:, at].astype(F32) + dot_nn(probability.astype(BF16), value_rows)
        return carry

    grad_rows = Gather(GR, gg, (gg.at[0, 0], gg.at[0, 1]))
    for h in (0, 1):
        grads.finish(h)
        grad_rows.to_right[h].start()
        grad_rows.to_left[h].start()
        lax.fori_loop(h * (H // 2), (h + 1) * (H // 2), attend, 0)

    whole = residual[...]
    centred = whole - jnp.mean(whole, axis=-1, keepdims=True)
    reciprocal = 1.0 / jnp.sqrt(jnp.mean(centred * centred, axis=-1, keepdims=True) + 1e-05)
    normed[...] = centred * reciprocal
    routed_in = (normed[...] * gain_ref[...]).astype(BF16)
    for h in (0, 1):
        send[1, h] = dot_nn(spread[h], routed_in[:, h * half : (h + 1) * half]).astype(BF16)
    rows = Exchange(AX, 1, xg.at[0], (along_z, along_xc))
    rows.first[0].start()
    rows.first[1].start()

    logits = dot_nt(routed_in, router_ref[...])
    first_logit = jnp.sum(jnp.where(first_hot, logits, 0.0), axis=-1, keepdims=True)
    second_logit = jnp.sum(jnp.where(second_hot, logits, 0.0), axis=-1, keepdims=True)
    gates = 1.0 / (1.0 + jnp.exp(second_logit - first_logit)), 1.0 / (1.0 + jnp.exp(first_logit - second_logit))

    hidden_units = win.shape[0]
    step = 256

    def prepare(d):
        def up(i, carry):
            at = pl.ds(pl.multiple_of(i * step, step), step)
            weight_out = wout[at, :]
            ready[d, :, at] = dot_nt(gg[d, 0], weight_out[:, :half]) + dot_nt(gg[d, 1], weight_out[:, half:])
            return carry

        lax.fori_loop(0, hidden_units // step, up, 0)

    def expert(d):
        def up(i, carry):
            at = pl.ds(pl.multiple_of(i * step, step), step)
            weight_in = win[at, :]
            signal = dot_nt(xg[d, 0], weight_in[:, :half]) + dot_nt(xg[d, 1], weight_in[:, half:])
            square = signal * signal
            tangent = jnp.tanh(gelu_scale * (signal + cubic_weight * signal * square))
            upper = 0.5 * (1.0 + tangent)
            hid[:, at] = (signal * upper).astype(BF16)
            slope = upper + 0.5 * signal * (1.0 - tangent * tangent) * gelu_scale * (1.0 + 3.0 * cubic_weight * square)
            ghd[:, at] = (ready[d, :, at] * slope).astype(BF16)
            return carry

        lax.fori_loop(0, hidden_units // step, up, 0)
        gate = jnp.zeros((SLOTS, 1), F32)
        for n in range(width // step):
            at = slice(n * step, (n + 1) * step)
            h, low = divmod(n * step, half)
            inner = slice(low, low + step)
            part[0, d, h, :, inner] = dot_nn(ghd[...], win[:, at]).astype(BF16)
            result = dot_nn(hid[...], wout[:, at])
            gate = gate + jnp.sum(result * gg[d, h, :, inner].astype(F32), axis=-1, keepdims=True)
            part[1, d, h, :, inner] = result.astype(BF16)
        gate_part[d] = jnp.broadcast_to(gate, (SLOTS, HD)).T[:8]

    sums = [Reduce(i, part.at[i], opp.at[i], near_l.at[i], near_r.at[i]) for i in (RG, RO)]
    gate_sums = [
        remote(gate_part.at[d], gate_near.at[d - 1], gate_s.at[d - 1], gate_r.at[d - 1], device)
        for d, device in ((1, right), (2, across), (3, left))
    ]
    row_gather = Gather(XR, xg, (xg.at[0, 0], xg.at[0, 1]))
    grad_rows.forward_right()
    own_out.wait()
    prepare(0)
    rows.middle(1)
    rows.middle(0)
    grad_rows.forward_left()
    for h in (0, 1):
        rows.finish(h)
        row_gather.to_right[h].start()
        row_gather.to_left[h].start()
    grad_rows.to_right[1].wait_recv()
    prepare(3)
    grad_rows.to_left[0].wait_recv()
    prepare(1)
    own_in.wait()

    expert(0)
    row_gather.forward_right()
    row_gather.forward_left()
    grad_rows.on_right.wait_recv()
    grad_rows.on_left.wait_recv()
    prepare(2)
    row_gather.to_right[1].wait_recv()
    expert(3)
    gate_sums[2].start()
    sums[RG].left_a.start()
    row_gather.to_left[0].wait_recv()
    expert(1)
    gate_sums[0].start()
    sums[RG].right_b.start()
    row_gather.on_right.wait_recv()
    row_gather.on_left.wait_recv()
    expert(2)
    gate_sums[1].start()
    sums[RG].opposite_a.start()
    sums[RG].opposite_b.start()
    sums[RG].pass_on()
    for copy in (sums[RO].opposite_a, sums[RO].opposite_b, sums[RO].right_b, sums[RO].left_a):
        copy.start()

    for copy in gate_sums:
        copy.wait_recv()
    gate_total = gate_part[0] + gate_near[0] + gate_near[1] + gate_near[2]
    rest = jnp.broadcast_to(gate_total[0:1], (HD, SLOTS)).T
    piece_lanes = lax.broadcasted_iota(jnp.int32, (SLOTS, HD), 1)
    packed = jnp.zeros((SLOTS, HD), F32)
    for n in range(3):
        piece = rest.astype(BF16).astype(F32)
        packed = packed + jnp.where(piece_lanes == n, piece, 0.0)
        rest = rest - piece
    gate_rows[0] = packed.astype(BF16)
    gate_first = Stage(16, gate_rows.at[0], gate_rows.at[1], xc_peer, xc)
    gate_second = Stage(17, gate_rows.at[2], gate_rows.at[3], z_peer, z)
    gate_first.start()

    def send_back(i):
        back = Exchange((BG, BO)[i], 2 + i, back_x.at[i], (along_xc, along_z))
        for h in (0, 1):
            total = part[i, 0, h].astype(F32) + near_l[i, h].astype(F32) + near_r[i, h].astype(F32)
            total = total.astype(BF16)
            send[2 + i, h] = total if h == 0 else dot_nn(swap_ref[...], total).astype(BF16)
            back.first[h].start()
        return back

    sums[RG].arrived()
    grads_back = send_back(RG)
    gate_first.arrived()
    turn(gate_rows.at[1], gate_rows.at[2])
    gate_second.start()
    grads_back.middle(0)
    grads_back.middle(1)
    sums[RO].pass_on()
    gate_second.arrived()
    grads_back.finish(0)
    grads_back.finish(1)

    cotangent = gout_ref[...].astype(F32)
    grad_routed, gate_grads = None, []
    for j in (0, 1):
        grad = gates[j] * jnp.concatenate([dot_nn(pick[j], back_x[RG, h]) for h in (0, 1)], axis=1)
        grad_routed = grad if grad_routed is None else grad_routed + grad
        gate_grads.append(jnp.sum(dot_nn(pick[j], gate_rows[3]), axis=-1, keepdims=True))
    gate_mean = gates[0] * gate_grads[0] + gates[1] * gate_grads[1]
    parts = [gates[j] * (gate_grads[j] - gate_mean) for j in (0, 1)]
    rest = jnp.where(first_hot, parts[0], 0.0) + jnp.where(second_hot, parts[1], 0.0)
    for _ in range(3):
        piece = rest.astype(BF16)
        grad_routed = grad_routed + dot_nn(piece, router_ref[...])
        rest = rest - piece.astype(F32)
    grad_norm = grad_routed * gain_ref[...]
    state = normed[...]
    grad_states = cotangent + reciprocal * (
        grad_norm
        - jnp.mean(grad_norm, axis=-1, keepdims=True)
        - state * jnp.mean(grad_norm * state, axis=-1, keepdims=True)
    )
    gstates_ref[...] = grad_states.astype(BF16)

    def value_grads(head, carry):
        at = columns(head)
        rows_of = dot_tn(prob[head].astype(BF16), gstates_ref[:, at]).astype(BF16)
        kpart[:, 1, :, at] = rows_of.reshape(ny, block_rows, HD)
        return carry

    def key_grads(head, carry):
        at = columns(head)
        value_rows = kvb[:, 1, :, at].reshape(sources, HD)
        probability = prob[head]
        grad_probability = dot_nt(gstates_ref[:, at], value_rows)
        inner = jnp.sum(probability * grad_probability, axis=-1, keepdims=True)
        grad_scores = (probability * (grad_probability - inner)).astype(BF16)
        slopes[head] = grad_scores
        rows_of = (dot_tn(grad_scores, q_ref[:, at]) * score_scale).astype(BF16)
        kpart[:, 0, :, at] = rows_of.reshape(ny, block_rows, HD)
        return carry

    def query_grads(head, carry):
        at = columns(head)
        key_rows = kvb[:, 0, :, at].reshape(sources, HD)
        gq_ref[:, at] = (dot_nn(slopes[head], key_rows) * score_scale).astype(BF16)
        return carry

    key_sum = Reduce(RKV, kpart, kopp, knear_l, knear_r)
    lax.fori_loop(0, H, value_grads, 0)
    key_sum.opposite_b.start()
    key_sum.right_b.start()
    sums[RO].arrived()
    outs_back = send_back(RO)
    lax.fori_loop(0, H, key_grads, 0)
    key_sum.opposite_a.start()
    key_sum.left_a.start()
    outs_back.middle(0)
    key_sum.pass_b()
    outs_back.middle(1)
    lax.fori_loop(0, H, query_grads, 0)
    key_sum.pass_a()
    outs_back.finish(0)
    outs_back.finish(1)
    outs = [jnp.concatenate([dot_nn(pick[j], back_x[RO, h]) for h in (0, 1)], axis=1) for j in (0, 1)]
    layer_ref[...] = (residual[...] + gates[0] * outs[0] + gates[1] * outs[1]).astype(BF16)
    key_sum.arrived()
    for h, out in ((0, gk_ref), (1, gv_ref)):
        out[...] = kpart[0, h].astype(F32) + knear_l[h].astype(F32) + knear_r[h].astype(F32)

    for gather in (keys, grad_rows, row_gather):
        gather.sent()
    for total in (*sums, key_sum):
        total.sent()
    for exchange in (grads, rows, grads_back, outs_back, gate_first, gate_second):
        exchange.sent()
    for copy in gate_sums:
        copy.wait_send()


def hand_over(*refs):
    count = len(refs) // 2
    for source, target in zip(refs[:count], refs[count:]):
        target[...] = source[...]


def swap_matrix():
    at = np.arange(SLOTS)
    outer, middle, inner = at // GROUP, at % GROUP // CAP, at % CAP
    matrix = np.zeros((SLOTS, SLOTS), np.float32)
    matrix[at, middle * GROUP + outer * CAP + inner] = 1.0
    return matrix


def on_device(dec, q, k, v, lengths, gain, router, ids, win, wout, gout):
    tokens, width = dec.shape[1:]
    block_rows = k.shape[1]
    hidden_units = win.shape[1]
    half = width // 2
    vmem = pl.BlockSpec(memory_space=pltpu.VMEM)
    hbm = pl.BlockSpec(memory_space=pl.ANY)
    shape = jax.ShapeDtypeStruct
    rows = (2, SLOTS, half)
    outs = pl.pallas_call(
        layer,
        out_shape=(
            shape((tokens, width), BF16),
            shape((tokens, width), BF16),
            shape((tokens, width), BF16),
            shape((block_rows, width), F32),
            shape((block_rows, width), F32),
        ),
        in_specs=[
            pl.BlockSpec(memory_space=pltpu.SMEM),
            vmem,
            vmem,
            hbm,
            hbm,
            vmem,
            vmem,
            vmem,
            hbm,
            hbm,
            vmem,
            vmem,
        ],
        out_specs=[vmem] * 5,
        scratch_shapes=[
            pltpu.VMEM((4, 2, block_rows, width), BF16),
            pltpu.VMEM((hidden_units, width), BF16),
            pltpu.VMEM((hidden_units, width), BF16),
            pltpu.VMEM((4, *rows), BF16),
            pltpu.VMEM((4, *rows), BF16),
            pltpu.VMEM((4, *rows), BF16),
            pltpu.VMEM((4, *rows), BF16),
            pltpu.VMEM((4, *rows), BF16),
            pltpu.VMEM((2, tokens, SLOTS), BF16),
            pltpu.VMEM((H, tokens, 4 * block_rows), F32),
            pltpu.VMEM((tokens, width), F32),
            pltpu.VMEM((tokens, width), F32),
            pltpu.VMEM((SLOTS, hidden_units), BF16),
            pltpu.VMEM((SLOTS, hidden_units), BF16),
            pltpu.VMEM((2, 4, *rows), BF16),
            pltpu.VMEM((2, *rows), BF16),
            pltpu.VMEM((2, *rows), BF16),
            pltpu.VMEM((2, *rows), BF16),
            pltpu.VMEM((4, 2, block_rows, width), BF16),
            pltpu.VMEM((2, block_rows, width), BF16),
            pltpu.VMEM((2, block_rows, width), BF16),
            pltpu.VMEM((2, block_rows, width), BF16),
            pltpu.VMEM((2, *rows), BF16),
            pltpu.VMEM((H, tokens, 4 * block_rows), BF16),
            pltpu.VMEM((4, 8, SLOTS), F32),
            pltpu.VMEM((3, 8, SLOTS), F32),
            pltpu.VMEM((4, SLOTS, HD), BF16),
            pltpu.VMEM((4, SLOTS, half), BF16),
            pltpu.VMEM((4, SLOTS, hidden_units), F32),
            pltpu.SemaphoreType.DMA((4,)),
            pltpu.SemaphoreType.DMA((18,)),
            pltpu.SemaphoreType.DMA((18,)),
            pltpu.SemaphoreType.DMA((18,)),
            pltpu.SemaphoreType.DMA((18,)),
            pltpu.SemaphoreType.DMA((18,)),
            pltpu.SemaphoreType.DMA((18,)),
            pltpu.SemaphoreType.DMA((3,)),
            pltpu.SemaphoreType.DMA((3,)),
        ],
        compiler_params=pltpu.CompilerParams(
            collective_id=0, has_side_effects=True, vmem_limit_bytes=62 * 2**20
        ),
        name="layer",
    )(
        lengths,
        dec[0],
        q[0],
        k[0],
        v[0],
        gain.reshape(1, width),
        router.T,
        ids[0].T,
        win[0],
        wout[0],
        gout[0],
        jnp.asarray(swap_matrix(), BF16),
    )
    count = len(outs)
    outs = pl.pallas_call(
        hand_over,
        out_shape=tuple(shape(out.shape, out.dtype) for out in outs),
        grid=(2,),
        in_specs=[pl.BlockSpec((out.shape[0] // 2, width), lambda i: (i, 0)) for out in outs],
        out_specs=[pl.BlockSpec((out.shape[0] // 2, width), lambda i: (i, 0)) for out in outs],
        name="hand_over",
    )(*outs)
    return tuple(out[None] for out in outs)


def solution(mesh):
    rows = P("expert", "seq", None)
    return jax.shard_map(
        on_device,
        mesh=mesh,
        in_specs=(rows, rows, rows, rows, P("expert"), P(), P(), rows, rows, rows, rows),
        out_specs=(rows,) * 5,
        check_vma=False,
    )
```

```python
import functools
import math

import jax
import jax.numpy as jnp
import numpy as np
from jax import lax
from jax.experimental import pallas as pl
from jax.experimental.pallas import tpu as pltpu
from jax.sharding import PartitionSpec as P

H = 8
HD = 128
CAP = 6
SIDE = 8
GROUP = SIDE * CAP
SLOTS = SIDE * GROUP
MESH = pl.DeviceIdType.MESH
F32 = jnp.float32
BF16 = jnp.bfloat16

gelu_scale = 0.7978845608028654
cubic_weight = 0.044715

KV, GR, XR = 0, 1, 2
RG, RO, RKV, RT = 0, 1, 2, 3
AG, AX, BG, BO = 0, 1, 2, 3


def dot_nn(a, b):
    return lax.dot_general(a, b, (((1,), (0,)), ((), ())), preferred_element_type=F32)


def dot_nt(a, b):
    return lax.dot_general(a, b, (((1,), (1,)), ((), ())), preferred_element_type=F32)


def dot_tn(a, b):
    return lax.dot_general(a, b, (((0,), (0,)), ((), ())), preferred_element_type=F32)


def layer(
    length_ref,
    dec_ref,
    q_ref,
    k_ref,
    v_ref,
    gain_ref,
    router_ref,
    ids_ref,
    win_ref,
    wout_ref,
    gout_ref,
    swap_ref,
    layer_ref,
    gstates_ref,
    gq_ref,
    gk_ref,
    gv_ref,
    kvb,
    win,
    wout,
    xg,
    gg,
    send,
    zbuf,
    turned,
    pick,
    prob,
    residual,
    normed,
    hid,
    ghd,
    part,
    opp,
    near_l,
    near_r,
    gpart,
    gopp,
    gnear_l,
    gnear_r,
    wide,
    far,
    tpart,
    topp,
    tnear_l,
    tnear_r,
    note,
    note_near,
    kpart,
    kopp,
    knear_l,
    knear_r,
    back_x,
    slopes,
    gate_part,
    gate_near,
    gate_rows,
    landed,
    ready,
    local_sem,
    ag_s,
    ag_r,
    rs_s,
    rs_r,
    xs_s,
    xs_r,
    gate_s,
    gate_r,
    note_s,
    note_r,
):
    tokens, width = dec_ref.shape
    half = width // 2
    ny = lax.axis_size("seq")
    y = lax.axis_index("seq")
    e = lax.axis_index("expert")
    core = lax.rem(e, 2)
    z = lax.rem(e // 2, SIDE)
    x = e // (2 * SIDE)
    xc = x * 2 + core
    right = (lax.rem(y + 1, ny), e)
    left = (lax.rem(y + ny - 1, ny), e)
    across = (lax.rem(y + 2, ny), e)
    hops = (4, 3, 5, 2, 6, 1, 7)

    def z_peer(hop):
        there = lax.rem(z + hop, SIDE)
        return there, (y, x * (2 * SIDE) + there * 2 + core)

    def xc_peer(hop):
        there = lax.rem(xc + hop, SIDE)
        return there, (y, (there // 2) * (2 * SIDE) + z * 2 + lax.rem(there, 2))

    def remote(src, dst, s, r, device):
        return pltpu.make_async_remote_copy(
            src_ref=src, dst_ref=dst, send_sem=s, recv_sem=r, device_id=device, device_id_type=MESH
        )

    own_k = pltpu.make_async_copy(k_ref, kvb.at[0, 0], local_sem.at[0])
    own_v = pltpu.make_async_copy(v_ref, kvb.at[0, 1], local_sem.at[1])
    own_in = pltpu.make_async_copy(win_ref, win, local_sem.at[2])
    own_out = pltpu.make_async_copy(wout_ref, wout, local_sem.at[3])
    for copy in (own_k, own_v, own_in, own_out):
        copy.start()

    barrier = pltpu.get_barrier_semaphore()
    for device in (left, right, across):
        pl.semaphore_signal(barrier, inc=1, device_id=device, device_id_type=MESH)
    for hop in hops:
        pl.semaphore_signal(barrier, inc=1, device_id=z_peer(hop)[1], device_id_type=MESH)
        pl.semaphore_signal(barrier, inc=1, device_id=xc_peer(hop)[1], device_id_type=MESH)

    class Gather:
        def __init__(self, number, buf, sources):
            def at(i):
                return ag_s.at[number * 6 + i], ag_r.at[number * 6 + i]

            self.to_right = [remote(sources[h], buf.at[3, h], *at(h), right) for h in (0, 1)]
            self.to_left = [remote(sources[h], buf.at[1, h], *at(2 + h), left) for h in (0, 1)]
            self.on_right = remote(buf.at[3, 0], buf.at[2, 0], *at(4), right)
            self.on_left = remote(buf.at[1, 1], buf.at[2, 1], *at(5), left)

        def forward_right(self):
            self.to_right[0].wait_recv()
            self.on_right.start()

        def forward_left(self):
            self.to_left[1].wait_recv()
            self.on_left.start()

        def sent(self):
            for copy in (*self.to_right, *self.to_left, self.on_right, self.on_left):
                copy.wait_send()

    class Reduce:
        def __init__(self, number, parts, crossed, from_left, from_right):
            def at(i):
                return rs_s.at[number * 6 + i], rs_r.at[number * 6 + i]

            self.parts, self.crossed = parts, crossed
            self.left_a = remote(parts.at[3, 0], from_right.at[0], *at(0), left)
            self.right_b = remote(parts.at[1, 1], from_left.at[1], *at(1), right)
            self.opposite_a = remote(parts.at[2, 0], crossed.at[0], *at(2), right)
            self.opposite_b = remote(parts.at[2, 1], crossed.at[1], *at(3), left)
            self.right_a = remote(parts.at[1, 0], from_left.at[0], *at(4), right)
            self.left_b = remote(parts.at[3, 1], from_right.at[1], *at(5), left)

        def pass_a(self):
            self.opposite_a.wait_recv()
            self.parts[1, 0] = (self.parts[1, 0].astype(F32) + self.crossed[0].astype(F32)).astype(BF16)
            self.right_a.start()

        def pass_b(self):
            self.opposite_b.wait_recv()
            self.parts[3, 1] = (self.parts[3, 1].astype(F32) + self.crossed[1].astype(F32)).astype(BF16)
            self.left_b.start()

        def pass_on(self):
            self.pass_a()
            self.pass_b()

        def arrived(self):
            for copy in (self.left_a, self.right_b, self.right_a, self.left_b):
                copy.wait_recv()

        def sent(self):
            for copy in (self.left_a, self.right_b, self.opposite_a, self.opposite_b, self.right_a, self.left_b):
                copy.wait_send()

    class Stage:
        def __init__(self, number, src, dst, peer, mine):
            self.s, self.r = xs_s.at[number], xs_r.at[number]
            self.src, self.dst, self.peer, self.mine = src, dst, peer, mine

        def rows(self, at):
            return pl.ds(pl.multiple_of(at * GROUP, 16), GROUP)

        def start(self):
            own = self.rows(self.mine)
            for hop in hops:
                there, device = self.peer(hop)
                remote(self.src.at[self.rows(there)], self.dst.at[own], self.s, self.r, device).start()
            pltpu.make_async_copy(self.src.at[own], self.dst.at[own], self.r).start()

        def arrived(self):
            pltpu.make_async_copy(self.src, self.dst, self.r).wait()

        def sent(self):
            most = pl.ds(0, SLOTS - GROUP)
            remote(self.src.at[most], self.dst.at[most], self.s, self.r, right).wait_send()

    def turn(src, dst):
        dst[...] = dot_nn(swap_ref[...], src[...]).astype(BF16)

    class Exchange:
        def __init__(self, number, tensor, dst, stages):
            here = (send, zbuf, turned)
            self.first, self.second, self.tensor, self.dst = [], [], tensor, dst
            for h in (0, 1):
                leave, between, go_on = (buf.at[tensor, h] for buf in here)
                end = dst.at[0] if h == 0 else landed.at[tensor]
                one, two = stages if h == 0 else stages[::-1]
                self.first.append(Stage(number * 4 + h, leave, between, *one))
                self.second.append(Stage(number * 4 + 2 + h, go_on, end, *two))

        def middle(self, h):
            self.first[h].arrived()
            turn(zbuf.at[self.tensor, h], turned.at[self.tensor, h])
            self.second[h].start()

        def finish(self, h):
            self.second[h].arrived()
            if h == 1:
                turn(landed.at[self.tensor], self.dst.at[1])

        def sent(self):
            for stage in (*self.first, *self.second):
                stage.sent()

    along_z, along_xc = (z_peer, z), (xc_peer, xc)

    experts = router_ref.shape[0]
    lanes = lax.broadcasted_iota(jnp.int32, (tokens, experts), 1)
    earlier = (
        lax.broadcasted_iota(jnp.int32, (tokens, tokens), 0) > lax.broadcasted_iota(jnp.int32, (tokens, tokens), 1)
    ).astype(F32).astype(BF16)
    slot_lanes = lax.broadcasted_iota(jnp.int32, (tokens, SLOTS), 1)
    base = ((lanes // 2) % SIDE) * GROUP + (lanes // (2 * SIDE)) * (2 * CAP) + (lanes % 2) * CAP

    def upright(row):
        return jnp.broadcast_to(row, (tokens, tokens)).T

    def choose(d, names):
        hot = [upright(names[j : j + 1]).astype(jnp.int32)[:, :experts] == lanes for j in (0, 1)]
        ones = [h.astype(F32) for h in hot]
        both = jnp.zeros((tokens, SLOTS), F32)
        for j in (0, 1):
            rank = dot_nn(earlier, ones[j].astype(BF16))
            if j == 1:
                rank = rank + jnp.sum(ones[0], axis=0, keepdims=True)
            slot = jnp.sum(ones[j] * (rank + base.astype(F32)), axis=-1, keepdims=True)
            chosen = (slot.astype(jnp.int32) == slot_lanes).astype(F32)
            pick[d, j] = chosen.astype(BF16)
            both = both + chosen
        return hot, both

    sublanes = lax.broadcasted_iota(jnp.int32, (8, tokens), 0)
    ids = [jnp.broadcast_to(ids_ref[j : j + 1, :].astype(F32), (8, tokens)) for j in (0, 1)]
    note[0] = jnp.where(sublanes == 0, ids[0], ids[1])
    (first_hot, second_hot), both = choose(0, note[0])
    spread = [both.T.astype(BF16)]
    spread.append(dot_nn(swap_ref[...], spread[0]).astype(BF16))
    for h in (0, 1):
        send[0, h] = dot_nn(spread[h], gout_ref[:, h * half : (h + 1) * half]).astype(BF16)

    pl.semaphore_wait(barrier, 3 + 2 * len(hops))
    notes = [
        remote(note.at[n], note_near.at[n, d - 1], note_s.at[n * 3 + d - 1], note_r.at[n * 3 + d - 1], device)
        for n in (0, 1)
        for d, device in ((1, left), (2, across), (3, right))
    ]
    keys = Gather(KV, kvb, (k_ref, v_ref))
    grads = Exchange(AG, 0, gg.at[0], (along_z, along_xc))
    keys.to_right[0].start()
    keys.to_left[1].start()
    grads.first[0].start()
    keys.to_right[1].start()
    keys.to_left[0].start()
    grads.first[1].start()
    for copy in notes[:3]:
        copy.start()
    keys.forward_right()
    keys.forward_left()
    grads.middle(1)
    grads.middle(0)
    keys.to_right[1].wait_recv()
    keys.to_left[0].wait_recv()
    own_k.wait()
    own_v.wait()
    keys.on_right.wait_recv()
    keys.on_left.wait_recv()

    score_scale = 1.0 / math.sqrt(HD)
    block_rows = kvb.shape[2]
    sources = ny * block_rows
    place = lax.broadcasted_iota(jnp.int32, (tokens, sources), 1)
    place = (place // block_rows + y) % ny * block_rows + place % block_rows
    valid = place < length_ref[0]

    def columns(head):
        return pl.ds(pl.multiple_of(head * HD, HD), HD)

    def attend(head, carry):
        at = columns(head)
        key_rows = kvb[:, 0, :, at].reshape(sources, HD)
        scores = dot_nt(q_ref[:, at], key_rows) * score_scale
        scores = jnp.where(valid, scores, -1e30)
        raw = jnp.exp(scores - jnp.max(scores, axis=-1, keepdims=True))
        probability = raw / jnp.sum(raw, axis=-1, keepdims=True)
        prob[head] = probability
        value_rows = kvb[:, 1, :, at].reshape(sources, HD)
        residual[:, at] = dec_ref[:, at].astype(F32) + dot_nn(probability.astype(BF16), value_rows)
        return carry

    grad_rows = Gather(GR, gg, (gg.at[0, 0], gg.at[0, 1]))
    for h in (0, 1):
        grads.finish(h)
        grad_rows.to_right[h].start()
        grad_rows.to_left[h].start()
        lax.fori_loop(h * (H // 2), (h + 1) * (H // 2), attend, 0)

    whole = residual[...]
    centred = whole - jnp.mean(whole, axis=-1, keepdims=True)
    reciprocal = 1.0 / jnp.sqrt(jnp.mean(centred * centred, axis=-1, keepdims=True) + 1e-05)
    normed[...] = centred * reciprocal
    routed_in = (normed[...] * gain_ref[...]).astype(BF16)
    for h in (0, 1):
        send[1, h] = dot_nn(spread[h], routed_in[:, h * half : (h + 1) * half]).astype(BF16)
    rows = Exchange(AX, 1, xg.at[0], (along_z, along_xc))
    rows.first[0].start()
    rows.first[1].start()

    logits = dot_nt(routed_in, router_ref[...])
    first_logit = jnp.sum(jnp.where(first_hot, logits, 0.0), axis=-1, keepdims=True)
    second_logit = jnp.sum(jnp.where(second_hot, logits, 0.0), axis=-1, keepdims=True)
    gates = 1.0 / (1.0 + jnp.exp(second_logit - first_logit)), 1.0 / (1.0 + jnp.exp(first_logit - second_logit))

    hidden_units = win.shape[0]
    step = 256

    def prepare(d):
        def up(i, carry):
            at = pl.ds(pl.multiple_of(i * step, step), step)
            weight_out = wout[at, :]
            ready[d, :, at] = dot_nt(gg[d, 0], weight_out[:, :half]) + dot_nt(gg[d, 1], weight_out[:, half:])
            return carry

        lax.fori_loop(0, hidden_units // step, up, 0)

    def expert(d):
        def up(i, carry):
            at = pl.ds(pl.multiple_of(i * step, step), step)
            weight_in = win[at, :]
            signal = dot_nt(xg[d, 0], weight_in[:, :half]) + dot_nt(xg[d, 1], weight_in[:, half:])
            square = signal * signal
            tangent = jnp.tanh(gelu_scale * (signal + cubic_weight * signal * square))
            upper = 0.5 * (1.0 + tangent)
            hid[:, at] = (signal * upper).astype(BF16)
            slope = upper + 0.5 * signal * (1.0 - tangent * tangent) * gelu_scale * (1.0 + 3.0 * cubic_weight * square)
            ghd[:, at] = (ready[d, :, at] * slope).astype(BF16)
            return carry

        lax.fori_loop(0, hidden_units // step, up, 0)
        gate = jnp.zeros((SLOTS, 1), F32)
        for n in range(width // step):
            at = slice(n * step, (n + 1) * step)
            h, low = divmod(n * step, half)
            inner = slice(low, low + step)
            grad = dot_nn(ghd[...], win[:, at]).astype(BF16)
            if h == 0:
                gpart[d, n] = grad
            else:
                wide[d, :, inner] = grad
            result = dot_nn(hid[...], wout[:, at])
            gate = gate + jnp.sum(result * gg[d, h, :, inner].astype(F32), axis=-1, keepdims=True)
            part[d, h, :, inner] = result.astype(BF16)
        gate_part[d] = jnp.broadcast_to(gate, (SLOTS, HD)).T[:8]

    sums = [
        Reduce(RG, gpart, gopp, gnear_l, gnear_r),
        Reduce(RO, part, opp, near_l, near_r),
    ]
    token_sum = Reduce(RT, tpart, topp, tnear_l, tnear_r)
    gate_sums = [
        remote(gate_part.at[d], gate_near.at[d - 1], gate_s.at[d - 1], gate_r.at[d - 1], device)
        for d, device in ((1, right), (2, across), (3, left))
    ]
    tall = [jnp.broadcast_to(gate, (tokens, tokens)).T[:8] for gate in gates]
    note[1] = jnp.where(sublanes == 0, tall[0], tall[1])
    for copy in notes[3:]:
        copy.start()
    row_gather = Gather(XR, xg, (xg.at[0, 0], xg.at[0, 1]))
    grad_rows.forward_right()
    for d in (1, 2, 3):
        notes[d - 1].wait_recv()
        choose(d, note_near[0, d - 1])
    own_out.wait()
    prepare(0)
    rows.middle(1)
    rows.middle(0)
    grad_rows.forward_left()
    for h in (0, 1):
        rows.finish(h)
        row_gather.to_right[h].start()
        row_gather.to_left[h].start()
    grad_rows.to_right[1].wait_recv()
    prepare(3)
    grad_rows.to_left[0].wait_recv()
    prepare(1)
    own_in.wait()

    halfway = [zbuf.at[2, 1], *(far.at[0, d] for d in range(3))]
    onward = [turned.at[2, 1], *(far.at[1, d] for d in range(3))]
    home = [landed.at[2], *(far.at[2, d] for d in range(3))]
    wide_first = [Stage(18 + 2 * d, wide.at[d], halfway[d], xc_peer, xc) for d in range(4)]
    wide_second = [Stage(19 + 2 * d, onward[d], home[d], z_peer, z) for d in range(4)]

    def go_on(d):
        wide_first[d].arrived()
        turn(halfway[d], onward[d])
        wide_second[d].start()

    def to_tokens(d):
        wide_second[d].arrived()
        rows_home = home[d][...]
        total = jnp.zeros((tokens, half), F32)
        for j in (0, 1):
            gate = gates[j] if d == 0 else upright(note_near[1, d - 1][j : j + 1])[:, 0:1]
            total = total + gate * dot_nn(pick[d, j], rows_home)
        for h in (0, 1):
            tpart[d, h] = total[:, h * (half // 2) : (h + 1) * (half // 2)].astype(BF16)

    expert(0)
    wide_first[0].start()
    row_gather.forward_right()
    row_gather.forward_left()
    grad_rows.on_right.wait_recv()
    grad_rows.on_left.wait_recv()
    prepare(2)
    row_gather.to_right[1].wait_recv()
    expert(3)
    gate_sums[2].start()
    sums[RG].left_a.start()
    wide_first[3].start()
    sums[RO].left_a.start()
    go_on(0)
    row_gather.to_left[0].wait_recv()
    expert(1)
    gate_sums[0].start()
    sums[RG].right_b.start()
    wide_first[1].start()
    sums[RO].right_b.start()
    go_on(3)
    row_gather.on_right.wait_recv()
    row_gather.on_left.wait_recv()
    expert(2)
    gate_sums[1].start()
    sums[RG].opposite_a.start()
    sums[RG].opposite_b.start()
    wide_first[2].start()
    sums[RO].opposite_a.start()
    sums[RO].opposite_b.start()
    go_on(1)
    for copy in notes[3:]:
        copy.wait_recv()
    to_tokens(0)
    go_on(2)
    sums[RG].pass_on()

    for copy in gate_sums:
        copy.wait_recv()
    gate_total = gate_part[0] + gate_near[0] + gate_near[1] + gate_near[2]
    rest = jnp.broadcast_to(gate_total[0:1], (HD, SLOTS)).T
    piece_lanes = lax.broadcasted_iota(jnp.int32, (SLOTS, HD), 1)
    packed = jnp.zeros((SLOTS, HD), F32)
    for n in range(3):
        piece = rest.astype(BF16).astype(F32)
        packed = packed + jnp.where(piece_lanes == n, piece, 0.0)
        rest = rest - piece
    gate_rows[0] = packed.astype(BF16)
    gate_first = Stage(16, gate_rows.at[0], gate_rows.at[1], xc_peer, xc)
    gate_second = Stage(17, gate_rows.at[2], gate_rows.at[3], z_peer, z)
    gate_first.start()

    to_tokens(3)
    token_sum.left_a.start()
    sums[RG].arrived()
    for h in (0, 1):
        total = gpart[0, h].astype(F32) + gnear_l[h].astype(F32) + gnear_r[h].astype(F32)
        send[2, 0, :, h * (half // 2) : (h + 1) * (half // 2)] = total.astype(BF16)
    narrow_first = Stage(BG * 4, send.at[2, 0], zbuf.at[2, 0], xc_peer, xc)
    narrow_second = Stage(BG * 4 + 2, turned.at[2, 0], back_x.at[0, 0], z_peer, z)
    narrow_first.start()
    gate_first.arrived()
    turn(gate_rows.at[1], gate_rows.at[2])
    gate_second.start()
    narrow_first.arrived()
    turn(zbuf.at[2, 0], turned.at[2, 0])
    narrow_second.start()
    to_tokens(1)
    token_sum.right_b.start()
    sums[RO].pass_on()
    to_tokens(2)
    token_sum.opposite_a.start()
    token_sum.opposite_b.start()
    token_sum.pass_on()
    gate_second.arrived()
    narrow_second.arrived()
    token_sum.arrived()

    cotangent = gout_ref[...].astype(F32)
    grad_routed = jnp.concatenate(
        [gates[0] * dot_nn(pick[0, 0], back_x[0, 0]) + gates[1] * dot_nn(pick[0, 1], back_x[0, 0])]
        + [tpart[0, h].astype(F32) + tnear_l[h].astype(F32) + tnear_r[h].astype(F32) for h in (0, 1)],
        axis=1,
    )
    gate_grads = [jnp.sum(dot_nn(pick[0, j], gate_rows[3]), axis=-1, keepdims=True) for j in (0, 1)]
    gate_mean = gates[0] * gate_grads[0] + gates[1] * gate_grads[1]
    parts = [gates[j] * (gate_grads[j] - gate_mean) for j in (0, 1)]
    rest = jnp.where(first_hot, parts[0], 0.0) + jnp.where(second_hot, parts[1], 0.0)
    for _ in range(3):
        piece = rest.astype(BF16)
        grad_routed = grad_routed + dot_nn(piece, router_ref[...])
        rest = rest - piece.astype(F32)
    grad_norm = grad_routed * gain_ref[...]
    state = normed[...]
    grad_states = cotangent + reciprocal * (
        grad_norm
        - jnp.mean(grad_norm, axis=-1, keepdims=True)
        - state * jnp.mean(grad_norm * state, axis=-1, keepdims=True)
    )
    gstates_ref[...] = grad_states.astype(BF16)

    def value_grads(head, carry):
        at = columns(head)
        rows_of = dot_tn(prob[head].astype(BF16), gstates_ref[:, at]).astype(BF16)
        kpart[:, 1, :, at] = rows_of.reshape(ny, block_rows, HD)
        return carry

    def key_grads(head, carry):
        at = columns(head)
        value_rows = kvb[:, 1, :, at].reshape(sources, HD)
        probability = prob[head]
        grad_probability = dot_nt(gstates_ref[:, at], value_rows)
        inner = jnp.sum(probability * grad_probability, axis=-1, keepdims=True)
        grad_scores = (probability * (grad_probability - inner)).astype(BF16)
        slopes[head] = grad_scores
        rows_of = (dot_tn(grad_scores, q_ref[:, at]) * score_scale).astype(BF16)
        kpart[:, 0, :, at] = rows_of.reshape(ny, block_rows, HD)
        return carry

    def query_grads(head, carry):
        at = columns(head)
        key_rows = kvb[:, 0, :, at].reshape(sources, HD)
        gq_ref[:, at] = (dot_nn(slopes[head], key_rows) * score_scale).astype(BF16)
        return carry

    key_sum = Reduce(RKV, kpart, kopp, knear_l, knear_r)
    lax.fori_loop(0, H, value_grads, 0)
    key_sum.opposite_b.start()
    key_sum.right_b.start()
    sums[RO].arrived()
    outs_back = Exchange(BO, 3, back_x.at[1], (along_xc, along_z))
    for h in (0, 1):
        total = part[0, h].astype(F32) + near_l[h].astype(F32) + near_r[h].astype(F32)
        total = total.astype(BF16)
        send[3, h] = total if h == 0 else dot_nn(swap_ref[...], total).astype(BF16)
        outs_back.first[h].start()
    lax.fori_loop(0, H, key_grads, 0)
    key_sum.opposite_a.start()
    key_sum.left_a.start()
    outs_back.middle(0)
    key_sum.pass_b()
    outs_back.middle(1)
    lax.fori_loop(0, H, query_grads, 0)
    key_sum.pass_a()
    outs_back.finish(0)
    outs_back.finish(1)
    outs = [jnp.concatenate([dot_nn(pick[0, j], back_x[1, h]) for h in (0, 1)], axis=1) for j in (0, 1)]
    layer_ref[...] = (residual[...] + gates[0] * outs[0] + gates[1] * outs[1]).astype(BF16)
    key_sum.arrived()
    for h, out in ((0, gk_ref), (1, gv_ref)):
        out[...] = kpart[0, h].astype(F32) + knear_l[h].astype(F32) + knear_r[h].astype(F32)

    for gather in (keys, grad_rows, row_gather):
        gather.sent()
    for total in (*sums, key_sum, token_sum):
        total.sent()
    for exchange in (grads, rows, outs_back, gate_first, gate_second, narrow_first, narrow_second, *wide_first, *wide_second):
        exchange.sent()
    for copy in (*gate_sums, *notes):
        copy.wait_send()


def hand_over(*refs):
    count = len(refs) // 2
    for source, target in zip(refs[:count], refs[count:]):
        target[...] = source[...]


def swap_matrix():
    at = np.arange(SLOTS)
    outer, middle, inner = at // GROUP, at % GROUP // CAP, at % CAP
    matrix = np.zeros((SLOTS, SLOTS), np.float32)
    matrix[at, middle * GROUP + outer * CAP + inner] = 1.0
    return matrix


def on_device(dec, q, k, v, lengths, gain, router, ids, win, wout, gout):
    tokens, width = dec.shape[1:]
    block_rows = k.shape[1]
    hidden_units = win.shape[1]
    half = width // 2
    vmem = pl.BlockSpec(memory_space=pltpu.VMEM)
    hbm = pl.BlockSpec(memory_space=pl.ANY)
    shape = jax.ShapeDtypeStruct
    rows = (2, SLOTS, half)
    outs = pl.pallas_call(
        layer,
        out_shape=(
            shape((tokens, width), BF16),
            shape((tokens, width), BF16),
            shape((tokens, width), BF16),
            shape((block_rows, width), F32),
            shape((block_rows, width), F32),
        ),
        in_specs=[
            pl.BlockSpec(memory_space=pltpu.SMEM),
            vmem,
            vmem,
            hbm,
            hbm,
            vmem,
            vmem,
            vmem,
            hbm,
            hbm,
            vmem,
            vmem,
        ],
        out_specs=[vmem] * 5,
        scratch_shapes=[
            pltpu.VMEM((4, 2, block_rows, width), BF16),
            pltpu.VMEM((hidden_units, width), BF16),
            pltpu.VMEM((hidden_units, width), BF16),
            pltpu.VMEM((4, *rows), BF16),
            pltpu.VMEM((4, *rows), BF16),
            pltpu.VMEM((4, *rows), BF16),
            pltpu.VMEM((4, *rows), BF16),
            pltpu.VMEM((4, *rows), BF16),
            pltpu.VMEM((4, 2, tokens, SLOTS), BF16),
            pltpu.VMEM((H, tokens, 4 * block_rows), F32),
            pltpu.VMEM((tokens, width), F32),
            pltpu.VMEM((tokens, width), F32),
            pltpu.VMEM((SLOTS, hidden_units), BF16),
            pltpu.VMEM((SLOTS, hidden_units), BF16),
            pltpu.VMEM((4, *rows), BF16),
            pltpu.VMEM(rows, BF16),
            pltpu.VMEM(rows, BF16),
            pltpu.VMEM(rows, BF16),
            pltpu.VMEM((4, 2, SLOTS, half // 2), BF16),
            pltpu.VMEM((2, SLOTS, half // 2), BF16),
            pltpu.VMEM((2, SLOTS, half // 2), BF16),
            pltpu.VMEM((2, SLOTS, half // 2), BF16),
            pltpu.VMEM((4, SLOTS, half), BF16),
            pltpu.VMEM((3, 3, SLOTS, half), BF16),
            pltpu.VMEM((4, 2, tokens, half // 2), BF16),
            pltpu.VMEM((2, tokens, half // 2), BF16),
            pltpu.VMEM((2, tokens, half // 2), BF16),
            pltpu.VMEM((2, tokens, half // 2), BF16),
            pltpu.VMEM((2, 8, tokens), F32),
            pltpu.VMEM((2, 3, 8, tokens), F32),
            pltpu.VMEM((4, 2, block_rows, width), BF16),
            pltpu.VMEM((2, block_rows, width), BF16),
            pltpu.VMEM((2, block_rows, width), BF16),
            pltpu.VMEM((2, block_rows, width), BF16),
            pltpu.VMEM((2, *rows), BF16),
            pltpu.VMEM((H, tokens, 4 * block_rows), BF16),
            pltpu.VMEM((4, 8, SLOTS), F32),
            pltpu.VMEM((3, 8, SLOTS), F32),
            pltpu.VMEM((4, SLOTS, HD), BF16),
            pltpu.VMEM((4, SLOTS, half), BF16),
            pltpu.VMEM((4, SLOTS, hidden_units), F32),
            pltpu.SemaphoreType.DMA((4,)),
            pltpu.SemaphoreType.DMA((18,)),
            pltpu.SemaphoreType.DMA((18,)),
            pltpu.SemaphoreType.DMA((24,)),
            pltpu.SemaphoreType.DMA((24,)),
            pltpu.SemaphoreType.DMA((26,)),
            pltpu.SemaphoreType.DMA((26,)),
            pltpu.SemaphoreType.DMA((3,)),
            pltpu.SemaphoreType.DMA((3,)),
            pltpu.SemaphoreType.DMA((6,)),
            pltpu.SemaphoreType.DMA((6,)),
        ],
        compiler_params=pltpu.CompilerParams(
            collective_id=0, has_side_effects=True, vmem_limit_bytes=62 * 2**20
        ),
        name="layer",
    )(
        lengths,
        dec[0],
        q[0],
        k[0],
        v[0],
        gain.reshape(1, width),
        router.T,
        ids[0].T,
        win[0],
        wout[0],
        gout[0],
        jnp.asarray(swap_matrix(), BF16),
    )
    count = len(outs)
    outs = pl.pallas_call(
        hand_over,
        out_shape=tuple(shape(out.shape, out.dtype) for out in outs),
        grid=(2,),
        in_specs=[pl.BlockSpec((out.shape[0] // 2, width), lambda i: (i, 0)) for out in outs],
        out_specs=[pl.BlockSpec((out.shape[0] // 2, width), lambda i: (i, 0)) for out in outs],
        name="hand_over",
    )(*outs)
    return tuple(out[None] for out in outs)


def solution(mesh):
    rows = P("expert", "seq", None)
    return jax.shard_map(
        on_device,
        mesh=mesh,
        in_specs=(rows, rows, rows, rows, P("expert"), P(), P(), rows, rows, rows, rows),
        out_specs=(rows,) * 5,
        check_vma=False,
    )
```

```python
import functools
import math

import jax
import jax.numpy as jnp
import numpy as np
from jax import lax
from jax.experimental import pallas as pl
from jax.experimental.pallas import tpu as pltpu
from jax.sharding import PartitionSpec as P

H = 8
HD = 128
CAP = 6
SIDE = 8
GROUP = SIDE * CAP
SLOTS = SIDE * GROUP
MESH = pl.DeviceIdType.MESH
F32 = jnp.float32
BF16 = jnp.bfloat16

gelu_scale = 0.7978845608028654
cubic_weight = 0.044715

KV, GR, XR = 0, 1, 2
RG, RO, RKV = 0, 1, 2
AG, AX, BG, BO = 0, 1, 2, 3


def dot_nn(a, b):
    return lax.dot_general(a, b, (((1,), (0,)), ((), ())), preferred_element_type=F32)


def dot_nt(a, b):
    return lax.dot_general(a, b, (((1,), (1,)), ((), ())), preferred_element_type=F32)


def dot_tn(a, b):
    return lax.dot_general(a, b, (((0,), (0,)), ((), ())), preferred_element_type=F32)


def layer(
    length_ref,
    dec_ref,
    q_ref,
    k_ref,
    v_ref,
    gain_ref,
    router_ref,
    ids_ref,
    win_ref,
    wout_ref,
    gout_ref,
    swap_ref,
    layer_ref,
    gstates_ref,
    gq_ref,
    gk_ref,
    gv_ref,
    kvb,
    win,
    wout,
    xg,
    gg,
    send,
    zbuf,
    turned,
    pick,
    prob,
    residual,
    normed,
    hid,
    ghd,
    part,
    opp,
    near_l,
    near_r,
    kpart,
    kopp,
    knear_l,
    knear_r,
    back_x,
    slopes,
    gate_part,
    gate_near,
    gate_rows,
    landed,
    ready,
    local_sem,
    ag_s,
    ag_r,
    rs_s,
    rs_r,
    xs_s,
    xs_r,
    gate_s,
    gate_r,
):
    tokens, width = dec_ref.shape
    half = width // 2
    ny = lax.axis_size("seq")
    y = lax.axis_index("seq")
    e = lax.axis_index("expert")
    core = lax.rem(e, 2)
    z = lax.rem(e // 2, SIDE)
    x = e // (2 * SIDE)
    xc = x * 2 + core
    right = (lax.rem(y + 1, ny), e)
    left = (lax.rem(y + ny - 1, ny), e)
    across = (lax.rem(y + 2, ny), e)
    hops = (4, 3, 5, 2, 6, 1, 7)

    def z_peer(hop):
        there = lax.rem(z + hop, SIDE)
        return there, (y, x * (2 * SIDE) + there * 2 + core)

    def xc_peer(hop):
        there = lax.rem(xc + hop, SIDE)
        return there, (y, (there // 2) * (2 * SIDE) + z * 2 + lax.rem(there, 2))

    def remote(src, dst, s, r, device):
        return pltpu.make_async_remote_copy(
            src_ref=src, dst_ref=dst, send_sem=s, recv_sem=r, device_id=device, device_id_type=MESH
        )

    own_k = pltpu.make_async_copy(k_ref, kvb.at[0, 0], local_sem.at[0])
    own_v = pltpu.make_async_copy(v_ref, kvb.at[0, 1], local_sem.at[1])
    own_in = pltpu.make_async_copy(win_ref, win, local_sem.at[2])
    own_out = pltpu.make_async_copy(wout_ref, wout, local_sem.at[3])
    for copy in (own_k, own_v, own_in, own_out):
        copy.start()

    barrier = pltpu.get_barrier_semaphore()
    for device in (left, right, across):
        pl.semaphore_signal(barrier, inc=1, device_id=device, device_id_type=MESH)
    for hop in hops:
        pl.semaphore_signal(barrier, inc=1, device_id=z_peer(hop)[1], device_id_type=MESH)
        pl.semaphore_signal(barrier, inc=1, device_id=xc_peer(hop)[1], device_id_type=MESH)

    class Gather:
        def __init__(self, number, buf, sources):
            def at(i):
                return ag_s.at[number * 6 + i], ag_r.at[number * 6 + i]

            self.to_right = [remote(sources[h], buf.at[3, h], *at(h), right) for h in (0, 1)]
            self.to_left = [remote(sources[h], buf.at[1, h], *at(2 + h), left) for h in (0, 1)]
            self.on_right = remote(buf.at[3, 0], buf.at[2, 0], *at(4), right)
            self.on_left = remote(buf.at[1, 1], buf.at[2, 1], *at(5), left)

        def forward_right(self):
            self.to_right[0].wait_recv()
            self.on_right.start()

        def forward_left(self):
            self.to_left[1].wait_recv()
            self.on_left.start()

        def sent(self):
            for copy in (*self.to_right, *self.to_left, self.on_right, self.on_left):
                copy.wait_send()

    class Reduce:
        def __init__(self, number, parts, crossed, from_left, from_right):
            def at(i):
                return rs_s.at[number * 6 + i], rs_r.at[number * 6 + i]

            self.parts, self.crossed = parts, crossed
            self.left_a = remote(parts.at[3, 0], from_right.at[0], *at(0), left)
            self.right_b = remote(parts.at[1, 1], from_left.at[1], *at(1), right)
            self.opposite_a = remote(parts.at[2, 0], crossed.at[0], *at(2), right)
            self.opposite_b = remote(parts.at[2, 1], crossed.at[1], *at(3), left)
            self.right_a = remote(parts.at[1, 0], from_left.at[0], *at(4), right)
            self.left_b = remote(parts.at[3, 1], from_right.at[1], *at(5), left)

        def pass_a(self):
            self.opposite_a.wait_recv()
            self.parts[1, 0] = (self.parts[1, 0].astype(F32) + self.crossed[0].astype(F32)).astype(BF16)
            self.right_a.start()

        def pass_b(self):
            self.opposite_b.wait_recv()
            self.parts[3, 1] = (self.parts[3, 1].astype(F32) + self.crossed[1].astype(F32)).astype(BF16)
            self.left_b.start()

        def pass_on(self):
            self.pass_a()
            self.pass_b()

        def arrived(self):
            for copy in (self.left_a, self.right_b, self.right_a, self.left_b):
                copy.wait_recv()

        def sent(self):
            for copy in (self.left_a, self.right_b, self.opposite_a, self.opposite_b, self.right_a, self.left_b):
                copy.wait_send()

    class Stage:
        def __init__(self, number, src, dst, peer, mine):
            self.s, self.r = xs_s.at[number], xs_r.at[number]
            self.src, self.dst, self.peer, self.mine = src, dst, peer, mine

        def rows(self, at):
            return pl.ds(pl.multiple_of(at * GROUP, 16), GROUP)

        def start(self):
            own = self.rows(self.mine)
            for hop in hops:
                there, device = self.peer(hop)
                remote(self.src.at[self.rows(there)], self.dst.at[own], self.s, self.r, device).start()
            pltpu.make_async_copy(self.src.at[own], self.dst.at[own], self.r).start()

        def arrived(self):
            pltpu.make_async_copy(self.src, self.dst, self.r).wait()

        def sent(self):
            most = pl.ds(0, SLOTS - GROUP)
            remote(self.src.at[most], self.dst.at[most], self.s, self.r, right).wait_send()

    def turn(src, dst):
        dst[...] = dot_nn(swap_ref[...], src[...]).astype(BF16)

    class Exchange:
        def __init__(self, number, tensor, dst, stages):
            here = (send, zbuf, turned)
            self.first, self.second, self.tensor, self.dst = [], [], tensor, dst
            for h in (0, 1):
                leave, between, go_on = (buf.at[tensor, h] for buf in here)
                end = dst.at[0] if h == 0 else landed.at[tensor]
                one, two = stages if h == 0 else stages[::-1]
                self.first.append(Stage(number * 4 + h, leave, between, *one))
                self.second.append(Stage(number * 4 + 2 + h, go_on, end, *two))

        def middle(self, h):
            self.first[h].arrived()
            turn(zbuf.at[self.tensor, h], turned.at[self.tensor, h])
            self.second[h].start()

        def finish(self, h):
            self.second[h].arrived()
            if h == 1:
                turn(landed.at[self.tensor], self.dst.at[1])

        def sent(self):
            for stage in (*self.first, *self.second):
                stage.sent()

    along_z, along_xc = (z_peer, z), (xc_peer, xc)

    experts = router_ref.shape[0]
    named = [
        jnp.broadcast_to(ids_ref[j : j + 1, :].astype(F32), (tokens, tokens)).T[:, :experts].astype(jnp.int32)
        for j in (0, 1)
    ]
    lanes = lax.broadcasted_iota(jnp.int32, (tokens, experts), 1)
    first_hot = named[0] == lanes
    second_hot = named[1] == lanes
    ones = first_hot.astype(F32), second_hot.astype(F32)
    earlier = (
        lax.broadcasted_iota(jnp.int32, (tokens, tokens), 0) > lax.broadcasted_iota(jnp.int32, (tokens, tokens), 1)
    ).astype(F32).astype(BF16)
    slot_lanes = lax.broadcasted_iota(jnp.int32, (tokens, SLOTS), 1)
    base = ((lanes // 2) % SIDE) * GROUP + (lanes // (2 * SIDE)) * (2 * CAP) + (lanes % 2) * CAP
    both = jnp.zeros((tokens, SLOTS), F32)
    for j in (0, 1):
        rank = dot_nn(earlier, ones[j].astype(BF16))
        if j == 1:
            rank = rank + jnp.sum(ones[0], axis=0, keepdims=True)
        slot = jnp.sum(ones[j] * (rank + base.astype(F32)), axis=-1, keepdims=True)
        chosen = (slot.astype(jnp.int32) == slot_lanes).astype(F32)
        pick[j] = chosen.astype(BF16)
        both = both + chosen
    spread = [both.T.astype(BF16)]
    spread.append(dot_nn(swap_ref[...], spread[0]).astype(BF16))
    for h in (0, 1):
        send[0, h] = dot_nn(spread[h], gout_ref[:, h * half : (h + 1) * half]).astype(BF16)

    pl.semaphore_wait(barrier, 3 + 2 * len(hops))
    keys = Gather(KV, kvb, (k_ref, v_ref))
    grads = Exchange(AG, 0, gg.at[0], (along_z, along_xc))
    keys.to_right[0].start()
    keys.to_left[1].start()
    grads.first[0].start()
    keys.to_right[1].start()
    keys.to_left[0].start()
    grads.first[1].start()
    keys.forward_right()
    keys.forward_left()
    grads.middle(1)
    grads.middle(0)
    keys.to_right[1].wait_recv()
    keys.to_left[0].wait_recv()
    own_k.wait()
    own_v.wait()
    keys.on_right.wait_recv()
    keys.on_left.wait_recv()

    score_scale = 1.0 / math.sqrt(HD)
    block_rows = kvb.shape[2]
    sources = ny * block_rows
    place = lax.broadcasted_iota(jnp.int32, (tokens, sources), 1)
    place = (place // block_rows + y) % ny * block_rows + place % block_rows
    valid = place < length_ref[0]

    def columns(head):
        return pl.ds(pl.multiple_of(head * HD, HD), HD)

    def attend(head, carry):
        at = columns(head)
        key_rows = kvb[:, 0, :, at].reshape(sources, HD)
        scores = dot_nt(q_ref[:, at], key_rows) * score_scale
        scores = jnp.where(valid, scores, -1e30)
        raw = jnp.exp(scores - jnp.max(scores, axis=-1, keepdims=True))
        probability = raw / jnp.sum(raw, axis=-1, keepdims=True)
        prob[head] = probability
        value_rows = kvb[:, 1, :, at].reshape(sources, HD)
        residual[:, at] = dec_ref[:, at].astype(F32) + dot_nn(probability.astype(BF16), value_rows)
        return carry

    grad_rows = Gather(GR, gg, (gg.at[0, 0], gg.at[0, 1]))
    for h in (0, 1):
        grads.finish(h)
        grad_rows.to_right[h].start()
        grad_rows.to_left[h].start()
        lax.fori_loop(h * (H // 2), (h + 1) * (H // 2), attend, 0)

    whole = residual[...]
    centred = whole - jnp.mean(whole, axis=-1, keepdims=True)
    reciprocal = 1.0 / jnp.sqrt(jnp.mean(centred * centred, axis=-1, keepdims=True) + 1e-05)
    normed[...] = centred * reciprocal
    routed_in = (normed[...] * gain_ref[...]).astype(BF16)
    for h in (0, 1):
        send[1, h] = dot_nn(spread[h], routed_in[:, h * half : (h + 1) * half]).astype(BF16)
    rows = Exchange(AX, 1, xg.at[0], (along_z, along_xc))
    rows.first[0].start()
    rows.first[1].start()

    logits = dot_nt(routed_in, router_ref[...])
    first_logit = jnp.sum(jnp.where(first_hot, logits, 0.0), axis=-1, keepdims=True)
    second_logit = jnp.sum(jnp.where(second_hot, logits, 0.0), axis=-1, keepdims=True)
    gates = 1.0 / (1.0 + jnp.exp(second_logit - first_logit)), 1.0 / (1.0 + jnp.exp(first_logit - second_logit))

    hidden_units = win.shape[0]
    step = 256

    def prepare(d):
        def up(i, carry):
            at = pl.ds(pl.multiple_of(i * step, step), step)
            weight_out = wout[at, :]
            ready[d, :, at] = dot_nt(gg[d, 0], weight_out[:, :half]) + dot_nt(gg[d, 1], weight_out[:, half:])
            return carry

        lax.fori_loop(0, hidden_units // step, up, 0)

    def rise(d):
        def up(i, carry):
            at = pl.ds(pl.multiple_of(i * step, step), step)
            weight_in = win[at, :]
            signal = dot_nt(xg[d, 0], weight_in[:, :half]) + dot_nt(xg[d, 1], weight_in[:, half:])
            square = signal * signal
            tangent = jnp.tanh(gelu_scale * (signal + cubic_weight * signal * square))
            upper = 0.5 * (1.0 + tangent)
            hid[:, at] = (signal * upper).astype(BF16)
            slope = upper + 0.5 * signal * (1.0 - tangent * tangent) * gelu_scale * (1.0 + 3.0 * cubic_weight * square)
            ghd[:, at] = (ready[d, :, at] * slope).astype(BF16)
            return carry

        lax.fori_loop(0, hidden_units // step, up, 0)
    def fall_grads(d):
        for n in range(width // step):
            at = slice(n * step, (n + 1) * step)
            h, low = divmod(n * step, half)
            part[0, d, h, :, low : low + step] = dot_nn(ghd[...], win[:, at]).astype(BF16)

    def fall_outs(d):
        gate = jnp.zeros((SLOTS, 1), F32)
        for n in range(width // step):
            at = slice(n * step, (n + 1) * step)
            h, low = divmod(n * step, half)
            inner = slice(low, low + step)
            result = dot_nn(hid[...], wout[:, at])
            gate = gate + jnp.sum(result * gg[d, h, :, inner].astype(F32), axis=-1, keepdims=True)
            part[1, d, h, :, inner] = result.astype(BF16)
        gate_part[d] = jnp.broadcast_to(gate, (SLOTS, HD)).T[:8]

    sums = [Reduce(i, part.at[i], opp.at[i], near_l.at[i], near_r.at[i]) for i in (RG, RO)]
    gate_sums = [
        remote(gate_part.at[d], gate_near.at[d - 1], gate_s.at[d - 1], gate_r.at[d - 1], device)
        for d, device in ((1, right), (2, across), (3, left))
    ]
    row_gather = Gather(XR, xg, (xg.at[0, 0], xg.at[0, 1]))
    grad_rows.forward_right()
    own_out.wait()
    prepare(0)
    rows.middle(1)
    rows.middle(0)
    grad_rows.forward_left()
    for h in (0, 1):
        rows.finish(h)
        row_gather.to_right[h].start()
        row_gather.to_left[h].start()
    grad_rows.to_right[1].wait_recv()
    prepare(3)
    grad_rows.to_left[0].wait_recv()
    prepare(1)
    own_in.wait()

    rise(0)
    fall_grads(0)
    row_gather.forward_right()
    fall_outs(0)
    row_gather.forward_left()
    grad_rows.on_right.wait_recv()
    grad_rows.on_left.wait_recv()
    prepare(2)
    row_gather.to_right[1].wait_recv()
    rise(3)
    fall_grads(3)
    sums[RG].left_a.start()
    fall_outs(3)
    gate_sums[2].start()
    row_gather.to_left[0].wait_recv()
    rise(1)
    fall_grads(1)
    sums[RG].right_b.start()
    fall_outs(1)
    gate_sums[0].start()
    row_gather.on_right.wait_recv()
    row_gather.on_left.wait_recv()
    rise(2)
    fall_grads(2)
    sums[RG].opposite_a.start()
    sums[RG].opposite_b.start()
    fall_outs(2)
    gate_sums[1].start()
    sums[RG].pass_on()
    for copy in (sums[RO].opposite_a, sums[RO].opposite_b, sums[RO].right_b, sums[RO].left_a):
        copy.start()

    for copy in gate_sums:
        copy.wait_recv()
    gate_total = gate_part[0] + gate_near[0] + gate_near[1] + gate_near[2]
    rest = jnp.broadcast_to(gate_total[0:1], (HD, SLOTS)).T
    piece_lanes = lax.broadcasted_iota(jnp.int32, (SLOTS, HD), 1)
    packed = jnp.zeros((SLOTS, HD), F32)
    for n in range(3):
        piece = rest.astype(BF16).astype(F32)
        packed = packed + jnp.where(piece_lanes == n, piece, 0.0)
        rest = rest - piece
    gate_rows[0] = packed.astype(BF16)
    gate_first = Stage(16, gate_rows.at[0], gate_rows.at[1], xc_peer, xc)
    gate_second = Stage(17, gate_rows.at[2], gate_rows.at[3], z_peer, z)
    gate_first.start()

    def send_back(i):
        back = Exchange((BG, BO)[i], 2 + i, back_x.at[i], (along_xc, along_z))
        for h in (0, 1):
            total = part[i, 0, h].astype(F32) + near_l[i, h].astype(F32) + near_r[i, h].astype(F32)
            total = total.astype(BF16)
            send[2 + i, h] = total if h == 0 else dot_nn(swap_ref[...], total).astype(BF16)
            back.first[h].start()
        return back

    sums[RG].arrived()
    grads_back = send_back(RG)
    gate_first.arrived()
    turn(gate_rows.at[1], gate_rows.at[2])
    gate_second.start()
    grads_back.middle(0)
    grads_back.middle(1)
    sums[RO].pass_on()
    gate_second.arrived()
    grads_back.finish(0)
    grads_back.finish(1)

    cotangent = gout_ref[...].astype(F32)
    grad_routed, gate_grads = None, []
    for j in (0, 1):
        grad = gates[j] * jnp.concatenate([dot_nn(pick[j], back_x[RG, h]) for h in (0, 1)], axis=1)
        grad_routed = grad if grad_routed is None else grad_routed + grad
        gate_grads.append(jnp.sum(dot_nn(pick[j], gate_rows[3]), axis=-1, keepdims=True))
    gate_mean = gates[0] * gate_grads[0] + gates[1] * gate_grads[1]
    parts = [gates[j] * (gate_grads[j] - gate_mean) for j in (0, 1)]
    rest = jnp.where(first_hot, parts[0], 0.0) + jnp.where(second_hot, parts[1], 0.0)
    for _ in range(3):
        piece = rest.astype(BF16)
        grad_routed = grad_routed + dot_nn(piece, router_ref[...])
        rest = rest - piece.astype(F32)
    grad_norm = grad_routed * gain_ref[...]
    state = normed[...]
    grad_states = cotangent + reciprocal * (
        grad_norm
        - jnp.mean(grad_norm, axis=-1, keepdims=True)
        - state * jnp.mean(grad_norm * state, axis=-1, keepdims=True)
    )
    gstates_ref[...] = grad_states.astype(BF16)

    def value_grads(head, carry):
        at = columns(head)
        rows_of = dot_tn(prob[head].astype(BF16), gstates_ref[:, at]).astype(BF16)
        kpart[:, 1, :, at] = rows_of.reshape(ny, block_rows, HD)
        return carry

    def key_grads(head, carry):
        at = columns(head)
        value_rows = kvb[:, 1, :, at].reshape(sources, HD)
        probability = prob[head]
        grad_probability = dot_nt(gstates_ref[:, at], value_rows)
        inner = jnp.sum(probability * grad_probability, axis=-1, keepdims=True)
        grad_scores = (probability * (grad_probability - inner)).astype(BF16)
        slopes[head] = grad_scores
        rows_of = (dot_tn(grad_scores, q_ref[:, at]) * score_scale).astype(BF16)
        kpart[:, 0, :, at] = rows_of.reshape(ny, block_rows, HD)
        return carry

    def query_grads(head, carry):
        at = columns(head)
        key_rows = kvb[:, 0, :, at].reshape(sources, HD)
        gq_ref[:, at] = (dot_nn(slopes[head], key_rows) * score_scale).astype(BF16)
        return carry

    key_sum = Reduce(RKV, kpart, kopp, knear_l, knear_r)
    lax.fori_loop(0, H, value_grads, 0)
    key_sum.opposite_b.start()
    key_sum.right_b.start()
    sums[RO].arrived()
    outs_back = send_back(RO)
    lax.fori_loop(0, H, key_grads, 0)
    key_sum.opposite_a.start()
    key_sum.left_a.start()
    outs_back.middle(0)
    key_sum.pass_b()
    outs_back.middle(1)
    lax.fori_loop(0, H, query_grads, 0)
    key_sum.pass_a()
    outs_back.finish(0)
    outs_back.finish(1)
    outs = [jnp.concatenate([dot_nn(pick[j], back_x[RO, h]) for h in (0, 1)], axis=1) for j in (0, 1)]
    layer_ref[...] = (residual[...] + gates[0] * outs[0] + gates[1] * outs[1]).astype(BF16)
    key_sum.arrived()
    for h, out in ((0, gk_ref), (1, gv_ref)):
        out[...] = kpart[0, h].astype(F32) + knear_l[h].astype(F32) + knear_r[h].astype(F32)

    for gather in (keys, grad_rows, row_gather):
        gather.sent()
    for total in (*sums, key_sum):
        total.sent()
    for exchange in (grads, rows, grads_back, outs_back, gate_first, gate_second):
        exchange.sent()
    for copy in gate_sums:
        copy.wait_send()


def hand_over(*refs):
    count = len(refs) // 2
    for source, target in zip(refs[:count], refs[count:]):
        target[...] = source[...]


def swap_matrix():
    at = np.arange(SLOTS)
    outer, middle, inner = at // GROUP, at % GROUP // CAP, at % CAP
    matrix = np.zeros((SLOTS, SLOTS), np.float32)
    matrix[at, middle * GROUP + outer * CAP + inner] = 1.0
    return matrix


def on_device(dec, q, k, v, lengths, gain, router, ids, win, wout, gout):
    tokens, width = dec.shape[1:]
    block_rows = k.shape[1]
    hidden_units = win.shape[1]
    half = width // 2
    vmem = pl.BlockSpec(memory_space=pltpu.VMEM)
    hbm = pl.BlockSpec(memory_space=pl.ANY)
    shape = jax.ShapeDtypeStruct
    rows = (2, SLOTS, half)
    outs = pl.pallas_call(
        layer,
        out_shape=(
            shape((tokens, width), BF16),
            shape((tokens, width), BF16),
            shape((tokens, width), BF16),
            shape((block_rows, width), F32),
            shape((block_rows, width), F32),
        ),
        in_specs=[
            pl.BlockSpec(memory_space=pltpu.SMEM),
            vmem,
            vmem,
            hbm,
            hbm,
            vmem,
            vmem,
            vmem,
            hbm,
            hbm,
            vmem,
            vmem,
        ],
        out_specs=[vmem] * 5,
        scratch_shapes=[
            pltpu.VMEM((4, 2, block_rows, width), BF16),
            pltpu.VMEM((hidden_units, width), BF16),
            pltpu.VMEM((hidden_units, width), BF16),
            pltpu.VMEM((4, *rows), BF16),
            pltpu.VMEM((4, *rows), BF16),
            pltpu.VMEM((4, *rows), BF16),
            pltpu.VMEM((4, *rows), BF16),
            pltpu.VMEM((4, *rows), BF16),
            pltpu.VMEM((2, tokens, SLOTS), BF16),
            pltpu.VMEM((H, tokens, 4 * block_rows), F32),
            pltpu.VMEM((tokens, width), F32),
            pltpu.VMEM((tokens, width), F32),
            pltpu.VMEM((SLOTS, hidden_units), BF16),
            pltpu.VMEM((SLOTS, hidden_units), BF16),
            pltpu.VMEM((2, 4, *rows), BF16),
            pltpu.VMEM((2, *rows), BF16),
            pltpu.VMEM((2, *rows), BF16),
            pltpu.VMEM((2, *rows), BF16),
            pltpu.VMEM((4, 2, block_rows, width), BF16),
            pltpu.VMEM((2, block_rows, width), BF16),
            pltpu.VMEM((2, block_rows, width), BF16),
            pltpu.VMEM((2, block_rows, width), BF16),
            pltpu.VMEM((2, *rows), BF16),
            pltpu.VMEM((H, tokens, 4 * block_rows), BF16),
            pltpu.VMEM((4, 8, SLOTS), F32),
            pltpu.VMEM((3, 8, SLOTS), F32),
            pltpu.VMEM((4, SLOTS, HD), BF16),
            pltpu.VMEM((4, SLOTS, half), BF16),
            pltpu.VMEM((4, SLOTS, hidden_units), F32),
            pltpu.SemaphoreType.DMA((4,)),
            pltpu.SemaphoreType.DMA((18,)),
            pltpu.SemaphoreType.DMA((18,)),
            pltpu.SemaphoreType.DMA((18,)),
            pltpu.SemaphoreType.DMA((18,)),
            pltpu.SemaphoreType.DMA((18,)),
            pltpu.SemaphoreType.DMA((18,)),
            pltpu.SemaphoreType.DMA((3,)),
            pltpu.SemaphoreType.DMA((3,)),
        ],
        compiler_params=pltpu.CompilerParams(
            collective_id=0, has_side_effects=True, vmem_limit_bytes=62 * 2**20
        ),
        name="layer",
    )(
        lengths,
        dec[0],
        q[0],
        k[0],
        v[0],
        gain.reshape(1, width),
        router.T,
        ids[0].T,
        win[0],
        wout[0],
        gout[0],
        jnp.asarray(swap_matrix(), BF16),
    )
    count = len(outs)
    outs = pl.pallas_call(
        hand_over,
        out_shape=tuple(shape(out.shape, out.dtype) for out in outs),
        grid=(2,),
        in_specs=[pl.BlockSpec((out.shape[0] // 2, width), lambda i: (i, 0)) for out in outs],
        out_specs=[pl.BlockSpec((out.shape[0] // 2, width), lambda i: (i, 0)) for out in outs],
        name="hand_over",
    )(*outs)
    return tuple(out[None] for out in outs)


def solution(mesh):
    rows = P("expert", "seq", None)
    return jax.shard_map(
        on_device,
        mesh=mesh,
        in_specs=(rows, rows, rows, rows, P("expert"), P(), P(), rows, rows, rows, rows),
        out_specs=(rows,) * 5,
        check_vma=False,
    )
```

```python
import functools
import math

import jax
import jax.numpy as jnp
import numpy as np
from jax import lax
from jax.experimental import pallas as pl
from jax.experimental.pallas import tpu as pltpu
from jax.sharding import PartitionSpec as P

H = 8
HD = 128
CAP = 6
SIDE = 8
GROUP = SIDE * CAP
SLOTS = SIDE * GROUP
MESH = pl.DeviceIdType.MESH
F32 = jnp.float32
BF16 = jnp.bfloat16

gelu_scale = 0.7978845608028654
cubic_weight = 0.044715

KV, GR, XR = 0, 1, 2
RG, RO, RKV = 0, 1, 2
AG, AX, BG, BO = 0, 1, 2, 3


def dot_nn(a, b):
    return lax.dot_general(a, b, (((1,), (0,)), ((), ())), preferred_element_type=F32)


def dot_nt(a, b):
    return lax.dot_general(a, b, (((1,), (1,)), ((), ())), preferred_element_type=F32)


def dot_tn(a, b):
    return lax.dot_general(a, b, (((0,), (0,)), ((), ())), preferred_element_type=F32)


def layer(
    length_ref,
    dec_ref,
    q_ref,
    k_ref,
    v_ref,
    gain_ref,
    router_ref,
    ids_ref,
    win_ref,
    wout_ref,
    gout_ref,
    swap_ref,
    layer_ref,
    gstates_ref,
    gq_ref,
    gk_ref,
    gv_ref,
    kvb,
    win,
    wout,
    xg,
    gg,
    send,
    zbuf,
    turned,
    pick,
    prob,
    residual,
    normed,
    hid,
    ghd,
    part,
    opp,
    near_l,
    near_r,
    kpart,
    kopp,
    knear_l,
    knear_r,
    back_x,
    slopes,
    gate_part,
    gate_near,
    gate_rows,
    landed,
    ready,
    local_sem,
    ag_s,
    ag_r,
    rs_s,
    rs_r,
    xs_s,
    xs_r,
    gate_s,
    gate_r,
):
    tokens, width = dec_ref.shape
    half = width // 2
    ny = lax.axis_size("seq")
    y = lax.axis_index("seq")
    e = lax.axis_index("expert")
    core = lax.rem(e, 2)
    z = lax.rem(e // 2, SIDE)
    x = e // (2 * SIDE)
    xc = x * 2 + core
    right = (lax.rem(y + 1, ny), e)
    left = (lax.rem(y + ny - 1, ny), e)
    across = (lax.rem(y + 2, ny), e)
    hops = (4, 3, 5, 2, 6, 1, 7)

    def z_peer(hop):
        there = lax.rem(z + hop, SIDE)
        return there, (y, x * (2 * SIDE) + there * 2 + core)

    def xc_peer(hop):
        there = lax.rem(xc + hop, SIDE)
        return there, (y, (there // 2) * (2 * SIDE) + z * 2 + lax.rem(there, 2))

    def remote(src, dst, s, r, device):
        return pltpu.make_async_remote_copy(
            src_ref=src, dst_ref=dst, send_sem=s, recv_sem=r, device_id=device, device_id_type=MESH
        )

    own_k = pltpu.make_async_copy(k_ref, kvb.at[0, 0], local_sem.at[0])
    own_v = pltpu.make_async_copy(v_ref, kvb.at[0, 1], local_sem.at[1])
    own_in = pltpu.make_async_copy(win_ref, win, local_sem.at[2])
    own_out = pltpu.make_async_copy(wout_ref, wout, local_sem.at[3])
    for copy in (own_k, own_v, own_in, own_out):
        copy.start()

    barrier = pltpu.get_barrier_semaphore()
    for device in (left, right, across):
        pl.semaphore_signal(barrier, inc=1, device_id=device, device_id_type=MESH)
    for hop in hops:
        pl.semaphore_signal(barrier, inc=1, device_id=z_peer(hop)[1], device_id_type=MESH)
        pl.semaphore_signal(barrier, inc=1, device_id=xc_peer(hop)[1], device_id_type=MESH)

    class Gather:
        def __init__(self, number, buf, sources):
            def at(i):
                return ag_s.at[number * 6 + i], ag_r.at[number * 6 + i]

            self.to_right = [remote(sources[h], buf.at[3, h], *at(h), right) for h in (0, 1)]
            self.to_left = [remote(sources[h], buf.at[1, h], *at(2 + h), left) for h in (0, 1)]
            self.on_right = remote(buf.at[3, 0], buf.at[2, 0], *at(4), right)
            self.on_left = remote(buf.at[1, 1], buf.at[2, 1], *at(5), left)

        def forward_right(self):
            self.to_right[0].wait_recv()
            self.on_right.start()

        def forward_left(self):
            self.to_left[1].wait_recv()
            self.on_left.start()

        def sent(self):
            for copy in (*self.to_right, *self.to_left, self.on_right, self.on_left):
                copy.wait_send()

    class Reduce:
        def __init__(self, number, parts, crossed, from_left, from_right):
            def at(i):
                return rs_s.at[number * 6 + i], rs_r.at[number * 6 + i]

            self.parts, self.crossed = parts, crossed
            self.left_a = remote(parts.at[3, 0], from_right.at[0], *at(0), left)
            self.right_b = remote(parts.at[1, 1], from_left.at[1], *at(1), right)
            self.opposite_a = remote(parts.at[2, 0], crossed.at[0], *at(2), right)
            self.opposite_b = remote(parts.at[2, 1], crossed.at[1], *at(3), left)
            self.right_a = remote(parts.at[1, 0], from_left.at[0], *at(4), right)
            self.left_b = remote(parts.at[3, 1], from_right.at[1], *at(5), left)

        def pass_a(self):
            self.opposite_a.wait_recv()
            self.parts[1, 0] = (self.parts[1, 0].astype(F32) + self.crossed[0].astype(F32)).astype(BF16)
            self.right_a.start()

        def pass_b(self):
            self.opposite_b.wait_recv()
            self.parts[3, 1] = (self.parts[3, 1].astype(F32) + self.crossed[1].astype(F32)).astype(BF16)
            self.left_b.start()

        def pass_on(self):
            self.pass_a()
            self.pass_b()

        def arrived(self):
            for copy in (self.left_a, self.right_b, self.right_a, self.left_b):
                copy.wait_recv()

        def sent(self):
            for copy in (self.left_a, self.right_b, self.opposite_a, self.opposite_b, self.right_a, self.left_b):
                copy.wait_send()

    class Stage:
        def __init__(self, number, src, dst, peer, mine):
            self.s, self.r = xs_s.at[number], xs_r.at[number]
            self.src, self.dst, self.peer, self.mine = src, dst, peer, mine

        def rows(self, at):
            return pl.ds(pl.multiple_of(at * GROUP, 16), GROUP)

        def start(self):
            own = self.rows(self.mine)
            for hop in hops:
                there, device = self.peer(hop)
                remote(self.src.at[self.rows(there)], self.dst.at[own], self.s, self.r, device).start()
            pltpu.make_async_copy(self.src.at[own], self.dst.at[own], self.r).start()

        def arrived(self):
            pltpu.make_async_copy(self.src, self.dst, self.r).wait()

        def sent(self):
            most = pl.ds(0, SLOTS - GROUP)
            remote(self.src.at[most], self.dst.at[most], self.s, self.r, right).wait_send()

    def turn(src, dst):
        dst[...] = dot_nn(swap_ref[...], src[...]).astype(BF16)

    class Exchange:
        def __init__(self, number, tensor, dst, stages):
            here = (send, zbuf, turned)
            self.first, self.second, self.tensor, self.dst = [], [], tensor, dst
            for h in (0, 1):
                leave, between, go_on = (buf.at[tensor, h] for buf in here)
                end = dst.at[0] if h == 0 else landed.at[tensor]
                one, two = stages if h == 0 else stages[::-1]
                self.first.append(Stage(number * 4 + h, leave, between, *one))
                self.second.append(Stage(number * 4 + 2 + h, go_on, end, *two))

        def middle(self, h):
            self.first[h].arrived()
            turn(zbuf.at[self.tensor, h], turned.at[self.tensor, h])
            self.second[h].start()

        def finish(self, h):
            self.second[h].arrived()
            if h == 1:
                turn(landed.at[self.tensor], self.dst.at[1])

        def sent(self):
            for stage in (*self.first, *self.second):
                stage.sent()

    along_z, along_xc = (z_peer, z), (xc_peer, xc)

    experts = router_ref.shape[0]
    named = [
        jnp.broadcast_to(ids_ref[j : j + 1, :].astype(F32), (tokens, tokens)).T[:, :experts].astype(jnp.int32)
        for j in (0, 1)
    ]
    lanes = lax.broadcasted_iota(jnp.int32, (tokens, experts), 1)
    first_hot = named[0] == lanes
    second_hot = named[1] == lanes
    ones = first_hot.astype(F32), second_hot.astype(F32)
    earlier = (
        lax.broadcasted_iota(jnp.int32, (tokens, tokens), 0) > lax.broadcasted_iota(jnp.int32, (tokens, tokens), 1)
    ).astype(F32).astype(BF16)
    slot_lanes = lax.broadcasted_iota(jnp.int32, (tokens, SLOTS), 1)
    base = ((lanes // 2) % SIDE) * GROUP + (lanes // (2 * SIDE)) * (2 * CAP) + (lanes % 2) * CAP
    both = jnp.zeros((tokens, SLOTS), F32)
    for j in (0, 1):
        rank = dot_nn(earlier, ones[j].astype(BF16))
        if j == 1:
            rank = rank + jnp.sum(ones[0], axis=0, keepdims=True)
        slot = jnp.sum(ones[j] * (rank + base.astype(F32)), axis=-1, keepdims=True)
        chosen = (slot.astype(jnp.int32) == slot_lanes).astype(F32)
        pick[j] = chosen.astype(BF16)
        both = both + chosen
    spread = [both.T.astype(BF16)]
    spread.append(dot_nn(swap_ref[...], spread[0]).astype(BF16))
    for h in (0, 1):
        send[0, h] = dot_nn(spread[h], gout_ref[:, h * half : (h + 1) * half]).astype(BF16)

    pl.semaphore_wait(barrier, 3 + 2 * len(hops))
    keys = Gather(KV, kvb, (k_ref, v_ref))
    grads = Exchange(AG, 0, gg.at[0], (along_z, along_xc))
    keys.to_right[0].start()
    keys.to_left[1].start()
    grads.first[0].start()
    keys.to_right[1].start()
    keys.to_left[0].start()
    grads.first[1].start()
    keys.forward_right()
    keys.forward_left()
    grads.middle(1)
    grads.middle(0)
    keys.to_right[1].wait_recv()
    keys.to_left[0].wait_recv()
    own_k.wait()
    own_v.wait()
    keys.on_right.wait_recv()
    keys.on_left.wait_recv()

    score_scale = 1.0 / math.sqrt(HD)
    block_rows = kvb.shape[2]
    sources = ny * block_rows
    place = lax.broadcasted_iota(jnp.int32, (tokens, sources), 1)
    place = (place // block_rows + y) % ny * block_rows + place % block_rows
    valid = place < length_ref[0]

    def columns(head):
        return pl.ds(pl.multiple_of(head * HD, HD), HD)

    def attend(head, carry):
        at = columns(head)
        key_rows = kvb[:, 0, :, at].reshape(sources, HD)
        scores = dot_nt(q_ref[:, at], key_rows) * score_scale
        scores = jnp.where(valid, scores, -1e30)
        raw = jnp.exp(scores - jnp.max(scores, axis=-1, keepdims=True))
        probability = raw / jnp.sum(raw, axis=-1, keepdims=True)
        prob[head] = probability
        value_rows = kvb[:, 1, :, at].reshape(sources, HD)
        residual[:, at] = dec_ref[:, at].astype(F32) + dot_nn(probability.astype(BF16), value_rows)
        return carry

    grad_rows = Gather(GR, gg, (gg.at[0, 0], gg.at[0, 1]))
    for h in (0, 1):
        grads.finish(h)
        grad_rows.to_right[h].start()
        grad_rows.to_left[h].start()
        lax.fori_loop(h * (H // 2), (h + 1) * (H // 2), attend, 0)

    whole = residual[...]
    centred = whole - jnp.mean(whole, axis=-1, keepdims=True)
    reciprocal = 1.0 / jnp.sqrt(jnp.mean(centred * centred, axis=-1, keepdims=True) + 1e-05)
    normed[...] = centred * reciprocal
    routed_in = (normed[...] * gain_ref[...]).astype(BF16)
    for h in (0, 1):
        send[1, h] = dot_nn(spread[h], routed_in[:, h * half : (h + 1) * half]).astype(BF16)
    rows = Exchange(AX, 1, xg.at[0], (along_z, along_xc))
    rows.first[0].start()
    rows.first[1].start()

    logits = dot_nt(routed_in, router_ref[...])
    first_logit = jnp.sum(jnp.where(first_hot, logits, 0.0), axis=-1, keepdims=True)
    second_logit = jnp.sum(jnp.where(second_hot, logits, 0.0), axis=-1, keepdims=True)
    gates = 1.0 / (1.0 + jnp.exp(second_logit - first_logit)), 1.0 / (1.0 + jnp.exp(first_logit - second_logit))

    hidden_units = win.shape[0]
    step = 256

    def prepare(d):
        def up(i, carry):
            at = pl.ds(pl.multiple_of(i * step, step), step)
            weight_out = wout[at, :]
            ready[d, :, at] = dot_nt(gg[d, 0], weight_out[:, :half]) + dot_nt(gg[d, 1], weight_out[:, half:])
            return carry

        lax.fori_loop(0, hidden_units // step, up, 0)

    def rise(d):
        def up(i, carry):
            at = pl.ds(pl.multiple_of(i * step, step), step)
            weight_in = win[at, :]
            signal = dot_nt(xg[d, 0], weight_in[:, :half]) + dot_nt(xg[d, 1], weight_in[:, half:])
            square = signal * signal
            tangent = jnp.tanh(gelu_scale * (signal + cubic_weight * signal * square))
            upper = 0.5 * (1.0 + tangent)
            hid[:, at] = (signal * upper).astype(BF16)
            slope = upper + 0.5 * signal * (1.0 - tangent * tangent) * gelu_scale * (1.0 + 3.0 * cubic_weight * square)
            ghd[:, at] = (ready[d, :, at] * slope).astype(BF16)
            return carry

        lax.fori_loop(0, hidden_units // step, up, 0)
    def fall_grads(d):
        for n in range(width // step):
            at = slice(n * step, (n + 1) * step)
            h, low = divmod(n * step, half)
            part[0, d, h, :, low : low + step] = dot_nn(ghd[...], win[:, at]).astype(BF16)

    def fall_outs(d):
        gate = jnp.zeros((SLOTS, 1), F32)
        for n in range(width // step):
            at = slice(n * step, (n + 1) * step)
            h, low = divmod(n * step, half)
            inner = slice(low, low + step)
            result = dot_nn(hid[...], wout[:, at])
            gate = gate + jnp.sum(result * gg[d, h, :, inner].astype(F32), axis=-1, keepdims=True)
            part[1, d, h, :, inner] = result.astype(BF16)
        gate_part[d] = jnp.broadcast_to(gate, (SLOTS, HD)).T[:8]

    sums = [Reduce(i, part.at[i], opp.at[i], near_l.at[i], near_r.at[i]) for i in (RG, RO)]
    gate_sums = [
        remote(gate_part.at[d], gate_near.at[d - 1], gate_s.at[d - 1], gate_r.at[d - 1], device)
        for d, device in ((1, right), (2, across), (3, left))
    ]
    row_gather = Gather(XR, xg, (xg.at[0, 0], xg.at[0, 1]))
    grad_rows.forward_right()
    own_out.wait()
    prepare(0)
    rows.middle(1)
    rows.middle(0)
    grad_rows.forward_left()
    for h in (0, 1):
        rows.finish(h)
        row_gather.to_right[h].start()
        row_gather.to_left[h].start()
    grad_rows.to_right[1].wait_recv()
    prepare(3)
    grad_rows.to_left[0].wait_recv()
    prepare(1)
    own_in.wait()

    rise(0)
    fall_grads(0)
    row_gather.forward_right()
    fall_outs(0)
    row_gather.forward_left()
    grad_rows.on_right.wait_recv()
    grad_rows.on_left.wait_recv()
    prepare(2)
    row_gather.to_right[1].wait_recv()
    rise(3)
    fall_grads(3)
    sums[RG].left_a.start()
    fall_outs(3)
    gate_sums[2].start()
    row_gather.to_left[0].wait_recv()
    rise(1)
    fall_grads(1)
    sums[RG].right_b.start()
    fall_outs(1)
    gate_sums[0].start()
    row_gather.on_right.wait_recv()
    row_gather.on_left.wait_recv()
    rise(2)
    fall_grads(2)
    sums[RG].opposite_a.start()
    sums[RG].opposite_b.start()
    fall_outs(2)
    gate_sums[1].start()
    sums[RG].pass_on()
    for copy in (sums[RO].opposite_a, sums[RO].opposite_b, sums[RO].right_b, sums[RO].left_a):
        copy.start()

    for copy in gate_sums:
        copy.wait_recv()
    gate_total = gate_part[0] + gate_near[0] + gate_near[1] + gate_near[2]
    rest = jnp.broadcast_to(gate_total[0:1], (HD, SLOTS)).T
    piece_lanes = lax.broadcasted_iota(jnp.int32, (SLOTS, HD), 1)
    packed = jnp.zeros((SLOTS, HD), F32)
    for n in range(3):
        piece = rest.astype(BF16).astype(F32)
        packed = packed + jnp.where(piece_lanes == n, piece, 0.0)
        rest = rest - piece
    gate_rows[0] = packed.astype(BF16)
    gate_first = Stage(16, gate_rows.at[0], gate_rows.at[1], xc_peer, xc)
    gate_second = Stage(17, gate_rows.at[2], gate_rows.at[3], z_peer, z)
    gate_first.start()

    def send_back(i):
        back = Exchange((BG, BO)[i], 2 + i, back_x.at[i], (along_xc, along_z))
        for h in (0, 1):
            total = part[i, 0, h].astype(F32) + near_l[i, h].astype(F32) + near_r[i, h].astype(F32)
            total = total.astype(BF16)
            send[2 + i, h] = total if h == 0 else dot_nn(swap_ref[...], total).astype(BF16)
            back.first[h].start()
        return back

    sums[RG].arrived()
    grads_back = send_back(RG)
    gate_first.arrived()
    turn(gate_rows.at[1], gate_rows.at[2])
    gate_second.start()
    grads_back.middle(0)
    grads_back.middle(1)
    sums[RO].pass_on()
    gate_second.arrived()
    grads_back.finish(0)
    grads_back.finish(1)

    cotangent = gout_ref[...].astype(F32)
    grad_routed, gate_grads = None, []
    for j in (0, 1):
        grad = gates[j] * jnp.concatenate([dot_nn(pick[j], back_x[RG, h]) for h in (0, 1)], axis=1)
        grad_routed = grad if grad_routed is None else grad_routed + grad
        gate_grads.append(jnp.sum(dot_nn(pick[j], gate_rows[3]), axis=-1, keepdims=True))
    gate_mean = gates[0] * gate_grads[0] + gates[1] * gate_grads[1]
    parts = [gates[j] * (gate_grads[j] - gate_mean) for j in (0, 1)]
    rest = jnp.where(first_hot, parts[0], 0.0) + jnp.where(second_hot, parts[1], 0.0)
    for _ in range(3):
        piece = rest.astype(BF16)
        grad_routed = grad_routed + dot_nn(piece, router_ref[...])
        rest = rest - piece.astype(F32)
    grad_norm = grad_routed * gain_ref[...]
    state = normed[...]
    grad_states = cotangent + reciprocal * (
        grad_norm
        - jnp.mean(grad_norm, axis=-1, keepdims=True)
        - state * jnp.mean(grad_norm * state, axis=-1, keepdims=True)
    )
    gstates_ref[...] = grad_states.astype(BF16)

    def value_grads(head, carry):
        at = columns(head)
        rows_of = dot_tn(prob[head].astype(BF16), gstates_ref[:, at]).astype(BF16)
        kpart[:, 1, :, at] = rows_of.reshape(ny, block_rows, HD)
        return carry

    def key_grads(head, carry):
        at = columns(head)
        value_rows = kvb[:, 1, :, at].reshape(sources, HD)
        probability = prob[head]
        grad_probability = dot_nt(gstates_ref[:, at], value_rows)
        inner = jnp.sum(probability * grad_probability, axis=-1, keepdims=True)
        grad_scores = (probability * (grad_probability - inner)).astype(BF16)
        slopes[head] = grad_scores
        rows_of = (dot_tn(grad_scores, q_ref[:, at]) * score_scale).astype(BF16)
        kpart[:, 0, :, at] = rows_of.reshape(ny, block_rows, HD)
        return carry

    def query_grads(head, carry):
        at = columns(head)
        key_rows = kvb[:, 0, :, at].reshape(sources, HD)
        gq_ref[:, at] = (dot_nn(slopes[head], key_rows) * score_scale).astype(BF16)
        return carry

    key_sum = Reduce(RKV, kpart, kopp, knear_l, knear_r)
    lax.fori_loop(0, H, value_grads, 0)
    key_sum.opposite_b.start()
    key_sum.right_b.start()
    sums[RO].arrived()
    outs_back = send_back(RO)
    lax.fori_loop(0, H, key_grads, 0)
    key_sum.opposite_a.start()
    key_sum.left_a.start()
    outs_back.middle(0)
    key_sum.pass_b()
    outs_back.middle(1)
    key_sum.pass_a()
    lax.fori_loop(0, H, query_grads, 0)
    outs_back.finish(0)
    outs_back.finish(1)
    outs = [jnp.concatenate([dot_nn(pick[j], back_x[RO, h]) for h in (0, 1)], axis=1) for j in (0, 1)]
    layer_ref[...] = (residual[...] + gates[0] * outs[0] + gates[1] * outs[1]).astype(BF16)
    key_sum.arrived()
    for h, out in ((0, gk_ref), (1, gv_ref)):
        out[...] = kpart[0, h].astype(F32) + knear_l[h].astype(F32) + knear_r[h].astype(F32)

    for gather in (keys, grad_rows, row_gather):
        gather.sent()
    for total in (*sums, key_sum):
        total.sent()
    for exchange in (grads, rows, grads_back, outs_back, gate_first, gate_second):
        exchange.sent()
    for copy in gate_sums:
        copy.wait_send()


def hand_over(*refs):
    count = len(refs) // 2
    for source, target in zip(refs[:count], refs[count:]):
        target[...] = source[...]


def swap_matrix():
    at = np.arange(SLOTS)
    outer, middle, inner = at // GROUP, at % GROUP // CAP, at % CAP
    matrix = np.zeros((SLOTS, SLOTS), np.float32)
    matrix[at, middle * GROUP + outer * CAP + inner] = 1.0
    return matrix


def on_device(dec, q, k, v, lengths, gain, router, ids, win, wout, gout):
    tokens, width = dec.shape[1:]
    block_rows = k.shape[1]
    hidden_units = win.shape[1]
    half = width // 2
    vmem = pl.BlockSpec(memory_space=pltpu.VMEM)
    hbm = pl.BlockSpec(memory_space=pl.ANY)
    shape = jax.ShapeDtypeStruct
    rows = (2, SLOTS, half)
    outs = pl.pallas_call(
        layer,
        out_shape=(
            shape((tokens, width), BF16),
            shape((tokens, width), BF16),
            shape((tokens, width), BF16),
            shape((block_rows, width), F32),
            shape((block_rows, width), F32),
        ),
        in_specs=[
            pl.BlockSpec(memory_space=pltpu.SMEM),
            vmem,
            vmem,
            hbm,
            hbm,
            vmem,
            vmem,
            vmem,
            hbm,
            hbm,
            vmem,
            vmem,
        ],
        out_specs=[vmem] * 5,
        scratch_shapes=[
            pltpu.VMEM((4, 2, block_rows, width), BF16),
            pltpu.VMEM((hidden_units, width), BF16),
            pltpu.VMEM((hidden_units, width), BF16),
            pltpu.VMEM((4, *rows), BF16),
            pltpu.VMEM((4, *rows), BF16),
            pltpu.VMEM((4, *rows), BF16),
            pltpu.VMEM((4, *rows), BF16),
            pltpu.VMEM((4, *rows), BF16),
            pltpu.VMEM((2, tokens, SLOTS), BF16),
            pltpu.VMEM((H, tokens, 4 * block_rows), F32),
            pltpu.VMEM((tokens, width), F32),
            pltpu.VMEM((tokens, width), F32),
            pltpu.VMEM((SLOTS, hidden_units), BF16),
            pltpu.VMEM((SLOTS, hidden_units), BF16),
            pltpu.VMEM((2, 4, *rows), BF16),
            pltpu.VMEM((2, *rows), BF16),
            pltpu.VMEM((2, *rows), BF16),
            pltpu.VMEM((2, *rows), BF16),
            pltpu.VMEM((4, 2, block_rows, width), BF16),
            pltpu.VMEM((2, block_rows, width), BF16),
            pltpu.VMEM((2, block_rows, width), BF16),
            pltpu.VMEM((2, block_rows, width), BF16),
            pltpu.VMEM((2, *rows), BF16),
            pltpu.VMEM((H, tokens, 4 * block_rows), BF16),
            pltpu.VMEM((4, 8, SLOTS), F32),
            pltpu.VMEM((3, 8, SLOTS), F32),
            pltpu.VMEM((4, SLOTS, HD), BF16),
            pltpu.VMEM((4, SLOTS, half), BF16),
            pltpu.VMEM((4, SLOTS, hidden_units), F32),
            pltpu.SemaphoreType.DMA((4,)),
            pltpu.SemaphoreType.DMA((18,)),
            pltpu.SemaphoreType.DMA((18,)),
            pltpu.SemaphoreType.DMA((18,)),
            pltpu.SemaphoreType.DMA((18,)),
            pltpu.SemaphoreType.DMA((18,)),
            pltpu.SemaphoreType.DMA((18,)),
            pltpu.SemaphoreType.DMA((3,)),
            pltpu.SemaphoreType.DMA((3,)),
        ],
        compiler_params=pltpu.CompilerParams(
            collective_id=0, has_side_effects=True, vmem_limit_bytes=62 * 2**20
        ),
        name="layer",
    )(
        lengths,
        dec[0],
        q[0],
        k[0],
        v[0],
        gain.reshape(1, width),
        router.T,
        ids[0].T,
        win[0],
        wout[0],
        gout[0],
        jnp.asarray(swap_matrix(), BF16),
    )
    count = len(outs)
    outs = pl.pallas_call(
        hand_over,
        out_shape=tuple(shape(out.shape, out.dtype) for out in outs),
        grid=(2,),
        in_specs=[pl.BlockSpec((out.shape[0] // 2, width), lambda i: (i, 0)) for out in outs],
        out_specs=[pl.BlockSpec((out.shape[0] // 2, width), lambda i: (i, 0)) for out in outs],
        name="hand_over",
    )(*outs)
    return tuple(out[None] for out in outs)


def solution(mesh):
    rows = P("expert", "seq", None)
    return jax.shard_map(
        on_device,
        mesh=mesh,
        in_specs=(rows, rows, rows, rows, P("expert"), P(), P(), rows, rows, rows, rows),
        out_specs=(rows,) * 5,
        check_vma=False,
    )
```
